256 devices in a mesh: row: 64 (over z, y, core), layer: 4 (over x).
Axes of the slice: x: 4, y: 4, z: 8, core: 2. Of those that a mesh axis runs over, the one named last changes fastest.
Arguments:
- weights: bfloat16 [8, 5120, 16384], P('layer', 'row'), may hold values from -46 to 46
- coeffs: bfloat16 [8, 5120, 512], P('layer', 'row'), may hold values from -3 to 3
- basis: bfloat16 [512, 16384], P(None, 'row'), may hold values from -0.25 to 0.25
- sketch_map: bfloat16 [8, 16384, 256], P('layer', 'row'), may hold values from -0.015625 to 0.015625
- ranks: int32 [8], replicated, may hold values from 32 to 256, as said below
Outputs:
- coefficients: float32 [8, 256, 16384], P('layer', None, 'row')
The draws below stay inside these ranges and needn't reach their ends.
Inputs may be any that keep to these rules, and one draw needn't show every extreme that they name: `ranks`: every rank lies between 32 and 256, and both ends are taken by some layer.
All inputs are finite; a program needn't handle non-finite values.
Results may differ from the reference program's by a relative error of at most 0.0048.
Values may be sent and summed in bfloat16 or wider, within the bound.
No kernel may reach another device: no remote copies, remote signals or barrier semaphores. Data moves between devices by JAX's collectives and lax.ppermute only.
A program may use at most 128 MiB of HBM per device.

```python
import math
import jax
import jax.numpy as jnp
from jax import lax

D = 5120
F = 16384
K = 512
S = 256
LAYERS = 8


def draw_weights(key, part):
    key = jax.random.fold_in(key, 11)
    key_base, key_rows, key_cols = jax.random.split(key, 3)
    position = jnp.arange(D, dtype=jnp.float32) / D
    row_scale = (3.0 ** position)[None, :, None] * jnp.exp(jax.random.uniform(key_rows, (LAYERS, D, 1), minval=0.0, maxval=math.log(4.0)))
    col_scale = jnp.exp(jax.random.uniform(key_cols, (LAYERS, 1, F), minval=0.0, maxval=math.log(10.0)))
    base = jnp.clip(jax.random.normal(key_base, (LAYERS, D, F)), -6.0, 6.0)
    return (base * row_scale * col_scale / 16.0).astype(jnp.bfloat16)


def draw_ranks(key, part):
    key = jax.random.fold_in(key, 23)
    key_values, key_order = jax.random.split(key)
    values = jax.random.randint(key_values, (LAYERS,), S // 8, S + 1)
    order = jax.random.permutation(key_order, LAYERS)
    values = values.at[order[0]].set(S)
    values = values.at[order[1]].set(S // 8)
    return values.astype(jnp.int32)


def level_of(key, shape, shards, low, largest):
    level, own = 1.0, jax.random.fold_in(key, 6)
    for dim, blocks in shards:
        heights = jnp.exp(jax.random.uniform(jax.random.fold_in(own, dim), (blocks,), jnp.float32, low / len(shards), largest / len(shards)))
        level = level * jnp.repeat(heights, shape[dim] // blocks).reshape([-1 if axis == dim else 1 for axis in range(len(shape))])
    return level


def bell_draw(rng, dims, width, limit, cuts=(), kind=jnp.bfloat16):
    loudness = level_of(rng, dims, cuts, -0.22, 0.18) if cuts else 1.0
    values = jax.random.normal(rng, dims, jnp.float32) * width * loudness
    return jnp.minimum(jnp.maximum(values, -limit), limit).astype(kind)


def setup_inputs(seed: int = 0) -> dict:
    seeds = jax.random.split(jax.random.key(seed), 6)
    weights = draw_weights(jax.random.fold_in(seeds[5], 71), 0)
    coeffs = bell_draw(seeds[1], (LAYERS, D, K), 0.5, 3.0, ((0, 4), (1, 64)))
    basis = bell_draw(seeds[2], (K, F), K ** -0.5, 0.25, ((1, 64),))
    sketch_map = bell_draw(seeds[3], (LAYERS, F, S), (F * LAYERS) ** -0.5, 0.015625, ((0, 4), (1, 64)))
    ranks = draw_ranks(jax.random.fold_in(seeds[5], 71), 0)
    return {"weights": weights, "coeffs": coeffs, "basis": basis, "sketch_map": sketch_map, "ranks": ranks}


def reference(weights, coeffs, basis, sketch_map, ranks):

    def rebuild(pair):
        weight_layer, coeff_layer = pair
        lowrank = jnp.dot(coeff_layer.astype(jnp.float32), basis.astype(jnp.float32), preferred_element_type=jnp.float32)
        return (weight_layer.astype(jnp.float32) - lowrank).astype(jnp.bfloat16)
    residual = lax.map(rebuild, (weights, coeffs))

    def add_layer(totals, pair):
        resid_layer, test_layer = pair
        return (totals + jnp.dot(resid_layer.astype(jnp.float32), test_layer.astype(jnp.float32), preferred_element_type=jnp.float32), None)
    sketch, _ = lax.scan(add_layer, jnp.zeros((D, S), jnp.float32), (residual, sketch_map))
    gram = jnp.dot(sketch.T, sketch, precision=lax.Precision.HIGHEST)
    factor = jnp.linalg.cholesky(gram)
    ortho = jax.scipy.linalg.solve_triangular(factor, sketch.T, lower=True).T.astype(jnp.bfloat16)

    def project(resid_layer):
        return jnp.dot(ortho.T.astype(jnp.float32), resid_layer.astype(jnp.float32), preferred_element_type=jnp.float32)
    projected = lax.map(project, residual)
    kept_rows = jnp.arange(S, dtype=jnp.int32)[None, :] < ranks[:, None]
    return jnp.where(kept_rows[:, :, None], projected, 0.0)
```

```python
import functools

import jax
import jax.numpy as jnp
from jax import lax
from jax.experimental import pallas as pl
from jax.experimental.pallas import tpu as pltpu
from jax.sharding import Mesh
from jax.sharding import PartitionSpec as P

ROW = ("z", "y", "c")
BLK = 64


def cut_kernel(w_ref, o_ref):
    groups, cols = o_ref.shape[0], o_ref.shape[3]
    for g in range(groups):
        o_ref[g, 0] = w_ref[0, :, g * cols : (g + 1) * cols]


def cut_by_owner(weights, groups, planes):
    lay, rows, width = weights.shape
    cols = width // (groups * planes)
    return pl.pallas_call(
        cut_kernel,
        grid=(lay, planes),
        in_specs=[pl.BlockSpec((1, rows, groups * cols), lambda l, z: (l, 0, z))],
        out_specs=pl.BlockSpec((groups, 1, rows, cols), lambda l, z: (0, l, 0, z)),
        out_shape=jax.ShapeDtypeStruct((groups, lay, rows, planes * cols), weights.dtype),
        name="cut_by_owner",
    )(weights)


def residual_kernel(w_ref, c_ref, b_ref, m_ref, r_ref, s_ref):
    groups, _, rows, cols = w_ref.shape
    low = jnp.dot(
        c_ref[:, 0].reshape(groups * rows, -1), b_ref[0], preferred_element_type=jnp.float32
    )
    res = w_ref[:, 0].reshape(groups * rows, cols).astype(jnp.float32) - low
    res = res.astype(jnp.bfloat16)
    r_ref[:, 0] = res.reshape(groups, rows, cols)
    part = jnp.dot(res, m_ref[0, 0], preferred_element_type=jnp.float32)
    first = (pl.program_id(0) == 0) & (pl.program_id(1) == 0)

    @pl.when(first)
    def _():
        s_ref[...] = part

    @pl.when(jnp.logical_not(first))
    def _():
        s_ref[...] += part


def residual_and_sketch(w, coeffs, basis, maps):
    groups, lay, rows, width = w.shape
    planes, rank, cols = basis.shape
    sw = maps.shape[3]
    return pl.pallas_call(
        residual_kernel,
        grid=(lay, planes),
        in_specs=[
            pl.BlockSpec((groups, 1, rows, cols), lambda l, z: (0, l, 0, z)),
            pl.BlockSpec((groups, 1, rows, rank), lambda l, z: (0, l, 0, 0)),
            pl.BlockSpec((1, rank, cols), lambda l, z: (z, 0, 0)),
            pl.BlockSpec((1, 1, cols, sw), lambda l, z: (z, l, 0, 0)),
        ],
        out_specs=[
            pl.BlockSpec((groups, 1, rows, cols), lambda l, z: (0, l, 0, z)),
            pl.BlockSpec((groups * rows, sw), lambda l, z: (0, 0)),
        ],
        out_shape=[
            jax.ShapeDtypeStruct(w.shape, jnp.bfloat16),
            jax.ShapeDtypeStruct((groups * rows, sw), jnp.float32),
        ],
        name="residual_and_sketch",
    )(w, coeffs, basis, maps)


def project_kernel(s_ref, r_ref, o_ref, hi_ref, lo_ref):
    groups, _, rows, cols = r_ref.shape

    @pl.when((pl.program_id(0) == 0) & (pl.program_id(1) == 0))
    def _():
        st = s_ref[...].T
        hi = st.astype(jnp.bfloat16)
        hi_ref[...] = hi
        lo_ref[...] = (st - hi.astype(jnp.float32)).astype(jnp.bfloat16)

    res = r_ref[:, 0].reshape(groups * rows, cols)
    o_ref[0, 0] = jnp.dot(hi_ref[...], res, preferred_element_type=jnp.float32) + jnp.dot(
        lo_ref[...], res, preferred_element_type=jnp.float32
    )


def project(sketch, residual, planes):
    groups, lay, rows, width = residual.shape
    cols = width // planes
    sw = sketch.shape[1]
    return pl.pallas_call(
        project_kernel,
        grid=(lay, planes),
        in_specs=[
            pl.BlockSpec((groups * rows, sw), lambda l, z: (0, 0)),
            pl.BlockSpec((groups, 1, rows, cols), lambda l, z: (0, l, 0, z)),
        ],
        out_specs=pl.BlockSpec((1, 1, sw, cols), lambda l, z: (z, l, 0, 0)),
        out_shape=jax.ShapeDtypeStruct((planes, lay, sw, cols), jnp.float32),
        scratch_shapes=[
            pltpu.VMEM((sw, groups * rows), jnp.bfloat16),
            pltpu.VMEM((sw, groups * rows), jnp.bfloat16),
        ],
        name="project",
    )(sketch, residual)


def dot32(a, b, dims=((1,), (0,))):
    return lax.dot_general(
        a, b, (dims, ((), ())), precision=lax.Precision.HIGHEST, preferred_element_type=jnp.float32
    )


def factor_block(a):
    n = a.shape[0]
    row = lax.broadcasted_iota(jnp.int32, (n, n), 0)
    col = lax.broadcasted_iota(jnp.int32, (n, n), 1)
    both = jnp.concatenate([a, jnp.where(row == col, 1.0, 0.0)], axis=1)
    below = lax.broadcasted_iota(jnp.int32, (n, 2 * n), 0)
    done = []
    for j in range(n):
        pivot = lax.rsqrt(both[j : j + 1, j : j + 1])
        line = both[j : j + 1, :] * pivot
        mult = both[:, j : j + 1] * pivot
        done.append(line)
        both = both - jnp.where(below > j, mult * line, 0.0)
    return jnp.concatenate(done, axis=0)[:, n:]


def inverse_factor_kernel(g_ref, o_ref, a_ref):
    n = g_ref.shape[0]
    a_ref[...] = g_ref[...]
    o_ref[...] = jnp.zeros_like(o_ref)
    for k in range(0, n, BLK):
        e = k + BLK
        inv = factor_block(a_ref[k:e, k:e])
        o_ref[k:e, k:e] = inv
        if k:
            o_ref[k:e, :k] = dot32(inv, o_ref[k:e, :k])
        if e < n:
            panel = dot32(a_ref[e:, k:e], inv, ((1,), (1,)))
            a_ref[e:, e:] -= dot32(panel, panel, ((1,), (1,)))
            o_ref[e:, :e] -= dot32(panel, o_ref[k:e, :e])


def inverse_factor(gram):
    return pl.pallas_call(
        inverse_factor_kernel,
        out_shape=jax.ShapeDtypeStruct(gram.shape, jnp.float32),
        scratch_shapes=[pltpu.VMEM(gram.shape, jnp.float32)],
        name="inverse_factor",
    )(gram)


def finish_kernel(ranks_ref, inv_ref, p_ref, o_ref):
    l = pl.program_id(0)
    out = dot32(inv_ref[...], p_ref[0])
    kept = lax.broadcasted_iota(jnp.int32, out.shape, 0) < ranks_ref[l]
    o_ref[0] = jnp.where(kept, out, 0.0)


def finish(ranks, inv, proj):
    lay, sw, cols = proj.shape
    return pl.pallas_call(
        finish_kernel,
        grid=(lay,),
        in_specs=[
            pl.BlockSpec(memory_space=pltpu.SMEM),
            pl.BlockSpec((sw, sw), lambda l: (0, 0)),
            pl.BlockSpec((1, sw, cols), lambda l: (l, 0, 0)),
        ],
        out_specs=pl.BlockSpec((1, sw, cols), lambda l: (l, 0, 0)),
        out_shape=jax.ShapeDtypeStruct(proj.shape, jnp.float32),
        name="finish",
    )(ranks, inv, proj)


def sum_over(x, axis, size):
    parts = [x] + [
        lax.ppermute(x, axis, [(i, (i + k) % size) for i in range(size)]) for k in range(1, size)
    ]
    return sum(parts[1:], parts[0])


def per_device(planes, groups, lines, weights, coeffs, basis, sketch_map, ranks):
    lay = weights.shape[0]
    sw = sketch_map.shape[2]
    cut = cut_by_owner(weights, groups, planes)
    res_in = lax.all_to_all(cut, ("y", "c"), 0, 0, tiled=True)
    all_coeffs = lax.all_gather(coeffs, ("y", "c"), axis=0)
    all_basis = lax.all_gather(basis, "z", axis=0)
    all_maps = lax.all_gather(sketch_map, "z", axis=0)
    residual, part = residual_and_sketch(res_in, all_coeffs, all_basis, all_maps)
    rows = part.shape[0] // groups
    part = lax.all_to_all(part.reshape(groups, rows, sw), ("y", "c"), 0, 0, tiled=True)
    own = sum_over(part.sum(0), "x", lines)
    sketch = lax.all_to_all(
        jnp.broadcast_to(own[None], (groups, rows, sw)), ("y", "c"), 0, 0, tiled=True
    ).reshape(groups * rows, sw)
    proj = lax.psum_scatter(project(sketch, residual, planes), "z", scatter_dimension=0)
    gram = dot32(sketch, sketch, ((0,), (0,)))
    gram = lax.all_to_all(gram.reshape(planes, sw // planes, sw), "z", 0, 0, tiled=True).sum(0)
    gram = lax.all_to_all(
        jnp.broadcast_to(gram[None], (planes, sw // planes, sw)), "z", 0, 0, tiled=True
    ).reshape(sw, sw)
    inv = inverse_factor(gram)
    ranks_here = lax.dynamic_slice_in_dim(ranks, lax.axis_index("x") * lay, lay)
    return finish(ranks_here, inv, proj)


def solution(mesh):
    wide, lines = mesh.devices.shape
    groups = 8
    planes = wide // groups
    fine = Mesh(mesh.devices.reshape(planes, groups // 2, 2, lines), ROW + ("x",))
    in_specs = (
        P("x", ROW, None),
        P("x", ROW, None),
        P(None, ROW),
        P("x", ROW, None),
        P(),
    )
    return jax.shard_map(
        functools.partial(per_device, planes, groups, lines),
        mesh=fine,
        in_specs=in_specs,
        out_specs=P("x", None, ROW),
        check_vma=False,
    )
```

```python
import functools

import jax
import jax.numpy as jnp
from jax import lax
from jax.experimental import pallas as pl
from jax.experimental.pallas import tpu as pltpu
from jax.sharding import Mesh
from jax.sharding import PartitionSpec as P

ROW = ("z", "y", "c")
CORES = 2
BLK = 128
STEP = 4
VMEM = 48 * 1024 * 1024
PARAMS = pltpu.CompilerParams(vmem_limit_bytes=VMEM)
SCALARS = pl.BlockSpec(memory_space=pltpu.SMEM)


def cut_kernel(cols, w_ref, o_ref):
    groups, wide = o_ref.shape[0], o_ref.shape[3]
    for z in range(wide // cols):
        for g in range(groups):
            at = (z * groups + g) * cols
            o_ref[g, :, :, z * cols : (z + 1) * cols] = w_ref[:, :, at : at + cols]


def cut_by_owner(weights, groups, planes):
    lay, rows, width = weights.shape
    cols = width // (groups * planes)
    step = 2
    return pl.pallas_call(
        functools.partial(cut_kernel, cols),
        grid=(planes // step,),
        in_specs=[pl.BlockSpec((lay, rows, groups * cols * step), lambda z: (0, 0, z))],
        out_specs=pl.BlockSpec((groups, lay, rows, cols * step), lambda z: (0, 0, 0, z)),
        out_shape=jax.ShapeDtypeStruct((groups, lay, rows, planes * cols), weights.dtype),
        compiler_params=PARAMS,
        name="cut_by_owner",
    )(weights)


def group_at(pos_ref, k, groups, sign):
    lines = groups // CORES
    y = lax.rem(pos_ref[0] + sign * (k // CORES) + lines, lines)
    c = lax.rem(pos_ref[1] + k % CORES, CORES)
    return y * CORES + c


def residual_kernel(pos_ref, w_ref, c_ref, d_ref, b_ref, m_ref, r_ref, *rest):
    groups, _, rows, _ = w_ref.shape
    s_refs, (acc_ref, all_ref) = rest[:groups], rest[groups:]
    step, _, cols = b_ref.shape
    layer, plane = pl.program_id(0), pl.program_id(1)
    tall = groups * rows

    @pl.when((layer == 0) & (plane == 0))
    def _():
        acc_ref[...] = jnp.zeros_like(acc_ref)

    @pl.when(plane == 0)
    def _():
        for k in range(groups):
            at = pl.multiple_of(group_at(pos_ref, k, groups, -1) * rows, 16)
            all_ref[pl.ds(at, rows)] = (c_ref, d_ref)[k % CORES][k // CORES, 0]

    total = None
    for i in range(step):
        here = slice(i * cols, (i + 1) * cols)
        low = jnp.dot(all_ref[...], b_ref[i], preferred_element_type=jnp.float32)
        w = w_ref[:, 0, :, here].reshape(tall, cols).astype(jnp.float32)
        res = (w - low).astype(jnp.bfloat16)
        r_ref[:, 0, :, here] = res.reshape(groups, rows, cols)
        part = jnp.dot(res, m_ref[i], preferred_element_type=jnp.float32)
        total = part if total is None else total + part
    acc_ref[...] += total

    @pl.when((layer == pl.num_programs(0) - 1) & (plane == pl.num_programs(1) - 1))
    def _():
        for k in range(groups):
            at = pl.multiple_of(group_at(pos_ref, k, groups, 1) * rows, 16)
            s_refs[k][...] = acc_ref[pl.ds(at, rows)]


def residual_and_sketch(pos, w, coeffs, others, maps_basis, rank):
    groups, lay, rows, width = w.shape
    planes, _, sw = maps_basis.shape
    cols = width // planes
    mine = pl.BlockSpec((groups // CORES, 1, rows, rank), lambda l, z: (0, l, 0, 0))
    return pl.pallas_call(
        residual_kernel,
        grid=(lay, planes // STEP),
        in_specs=[
            SCALARS,
            pl.BlockSpec((groups, 1, rows, cols * STEP), lambda l, z: (0, l, 0, z)),
            mine,
            mine,
            pl.BlockSpec((STEP, rank, cols), lambda l, z: (z, 1, 0)),
            pl.BlockSpec((STEP, cols, sw), lambda l, z: (z, l, 0)),
        ],
        out_specs=[pl.BlockSpec((groups, 1, rows, cols * STEP), lambda l, z: (0, l, 0, z))]
        + [pl.BlockSpec((rows, sw), lambda l, z: (0, 0))] * groups,
        out_shape=[jax.ShapeDtypeStruct(w.shape, jnp.bfloat16)]
        + [jax.ShapeDtypeStruct((rows, sw), jnp.float32)] * groups,
        scratch_shapes=[
            pltpu.VMEM((groups * rows, sw), jnp.float32),
            pltpu.VMEM((groups * rows, rank), jnp.bfloat16),
        ],
        compiler_params=PARAMS,
        name="residual_and_sketch",
    )(pos, w, coeffs, others, maps_basis, maps_basis)


def gram_kernel(pos_ref, *refs):
    both_ref, g_ref, s_ref = refs[-3:]
    parts = refs[:-3]
    groups = len(parts)
    rows, sw = parts[0].shape
    for k in range(groups):
        at = pl.multiple_of(group_at(pos_ref, k, groups, -1) * rows, 16)
        s_ref[pl.ds(at, rows)] = parts[k][...]
    st = s_ref[...].T
    g_ref[...] = dot32(st, s_ref[...])
    high = st.astype(jnp.bfloat16)
    both_ref[:sw] = high
    both_ref[sw:] = (st - high.astype(jnp.float32)).astype(jnp.bfloat16)


def stack_and_gram(pos, parts):
    rows, sw = parts[0].shape
    tall = rows * len(parts)
    return pl.pallas_call(
        gram_kernel,
        in_specs=[SCALARS] + [pl.BlockSpec((rows, sw), lambda: (0, 0))] * len(parts),
        out_shape=[
            jax.ShapeDtypeStruct((2 * sw, tall), jnp.bfloat16),
            jax.ShapeDtypeStruct((sw, sw), jnp.float32),
        ],
        scratch_shapes=[pltpu.VMEM((tall, sw), jnp.float32)],
        compiler_params=PARAMS,
        name="stack_and_gram",
    )(pos, *parts)


def project_kernel(both_ref, r_ref, o_ref):
    groups, _, rows, wide = r_ref.shape
    step, _, sw, cols = o_ref.shape
    for i in range(step):
        res = r_ref[:, 0, :, i * cols : (i + 1) * cols].reshape(groups * rows, cols)
        out = jnp.dot(both_ref[...], res, preferred_element_type=jnp.float32)
        o_ref[i, 0] = out[:sw] + out[sw:]


def project(both, residual, planes):
    groups, lay, rows, width = residual.shape
    cols = width // planes
    sw = both.shape[0] // 2
    return pl.pallas_call(
        project_kernel,
        grid=(lay, planes // STEP),
        in_specs=[
            pl.BlockSpec(both.shape, lambda l, z: (0, 0)),
            pl.BlockSpec((groups, 1, rows, cols * STEP), lambda l, z: (0, l, 0, z)),
        ],
        out_specs=pl.BlockSpec((STEP, 1, sw, cols), lambda l, z: (z, l, 0, 0)),
        out_shape=jax.ShapeDtypeStruct((planes, lay, sw, cols), jnp.float32),
        compiler_params=PARAMS,
        name="project",
    )(both, residual)


def dot32(a, b, dims=((1,), (0,))):
    return lax.dot_general(
        a, b, (dims, ((), ())), precision=lax.Precision.HIGHEST, preferred_element_type=jnp.float32
    )


def factor_block(a):
    n = a.shape[0]
    row = lax.broadcasted_iota(jnp.int32, (n, n), 0)
    col = lax.broadcasted_iota(jnp.int32, (n, n), 1)
    both = jnp.concatenate([a, jnp.where(row == col, 1.0, 0.0)], axis=1)
    done = []
    for j in range(n):
        r = j % 8
        if j and r == 0:
            both = both[8:]
        pivot = lax.rsqrt(both[r : r + 1, j : j + 1])
        line = both[r : r + 1, :] * pivot
        mult = both[:, j : j + 1] * pivot
        done.append(line)
        if r < 7:
            keep = lax.broadcasted_iota(jnp.int32, (both.shape[0], 1), 0) > r
            mult = jnp.where(keep, mult, 0.0)
        both = both - mult * line
    return jnp.concatenate(done, axis=0)[:, n:]


def inverse_factor_kernel(g_ref, o_ref, a_ref):
    n = g_ref.shape[0]
    a_ref[...] = g_ref[...]
    o_ref[...] = jnp.zeros_like(o_ref)
    for k in range(0, n, BLK):
        e = k + BLK
        inv = factor_block(a_ref[k:e, k:e])
        o_ref[k:e, k:e] = inv
        if k:
            o_ref[k:e, :k] = dot32(inv, o_ref[k:e, :k])
        if e < n:
            panel = dot32(a_ref[e:, k:e], inv, ((1,), (1,)))
            a_ref[e:, e:] -= dot32(panel, panel, ((1,), (1,)))
            o_ref[e:, :e] -= dot32(panel, o_ref[k:e, :e])


def inverse_factor(gram):
    return pl.pallas_call(
        inverse_factor_kernel,
        out_shape=jax.ShapeDtypeStruct(gram.shape, jnp.float32),
        scratch_shapes=[pltpu.VMEM(gram.shape, jnp.float32)],
        compiler_params=PARAMS,
        name="inverse_factor",
    )(gram)


def finish_kernel(ranks_ref, inv_ref, p_ref, o_ref):
    l = pl.program_id(0)
    out = dot32(inv_ref[...], p_ref[0])
    kept = lax.broadcasted_iota(jnp.int32, out.shape, 0) < ranks_ref[l]
    o_ref[0] = jnp.where(kept, out, 0.0)


def finish(ranks, inv, proj):
    lay, sw, cols = proj.shape
    return pl.pallas_call(
        finish_kernel,
        grid=(lay,),
        in_specs=[
            SCALARS,
            pl.BlockSpec((sw, sw), lambda l: (0, 0)),
            pl.BlockSpec((1, sw, cols), lambda l: (l, 0, 0)),
        ],
        out_specs=pl.BlockSpec((1, sw, cols), lambda l: (l, 0, 0)),
        out_shape=jax.ShapeDtypeStruct(proj.shape, jnp.float32),
        compiler_params=PARAMS,
        name="finish",
    )(ranks, inv, proj)


def shift(x, axis, size, k):
    return lax.ppermute(x, axis, [(i, (i + k) % size) for i in range(size)])


def shift_group(x, groups, k):
    lines = groups // CORES
    pairs = [
        (y * CORES + c, (y + k // CORES) % lines * CORES + (c + k) % CORES)
        for y in range(lines)
        for c in range(CORES)
    ]
    return lax.ppermute(x, ("y", "c"), pairs)


def added(parts):
    return sum(parts[1:], parts[0])


def per_device(planes, groups, lines, weights, coeffs, basis, sketch_map, ranks):
    lay, _, _ = weights.shape
    sw = sketch_map.shape[2]
    ys = groups // CORES
    pos = jnp.stack([lax.axis_index("y"), lax.axis_index("c")]).astype(jnp.int32)
    own = jnp.concatenate([sketch_map.reshape(-1, sw), basis], axis=0)
    maps_basis = lax.all_gather(own, "z", axis=0)
    near = jnp.stack([coeffs] + [shift(coeffs, "y", ys, k) for k in range(1, ys)])
    others = shift(near, "c", CORES, 1)
    cut = cut_by_owner(weights, groups, planes)
    res_in = lax.all_to_all(cut, ("y", "c"), 0, 0, tiled=True)
    residual, *parts = residual_and_sketch(pos, res_in, near, others, maps_basis, basis.shape[0])
    mine = added([parts[0]] + [shift_group(parts[k], groups, k) for k in range(1, groups)])
    mine = added([mine] + [shift(mine, "x", lines, k) for k in range(1, lines)])
    rows_of = [mine] + [shift_group(mine, groups, k) for k in range(1, groups)]
    both, gram = stack_and_gram(pos, rows_of)
    proj = lax.psum_scatter(project(both, residual, planes), "z", scatter_dimension=0)
    gram = lax.all_to_all(gram.reshape(planes, sw // planes, sw), "z", 0, 0, tiled=True).sum(0)
    gram = lax.all_to_all(
        jnp.broadcast_to(gram[None], (planes, sw // planes, sw)), "z", 0, 0, tiled=True
    ).reshape(sw, sw)
    inv = inverse_factor(gram)
    ranks_here = lax.dynamic_slice_in_dim(ranks, lax.axis_index("x") * lay, lay)
    return finish(ranks_here, inv, proj)


def solution(mesh):
    wide, lines = mesh.devices.shape
    groups = 8
    planes = wide // groups
    fine = Mesh(mesh.devices.reshape(planes, groups // CORES, CORES, lines), ROW + ("x",))
    in_specs = (
        P("x", ROW, None),
        P("x", ROW, None),
        P(None, ROW),
        P("x", ROW, None),
        P(),
    )
    return jax.shard_map(
        functools.partial(per_device, planes, groups, lines),
        mesh=fine,
        in_specs=in_specs,
        out_specs=P("x", None, ROW),
        check_vma=False,
    )
```

```python
import functools

import jax
import jax.numpy as jnp
from jax import lax
from jax.experimental import pallas as pl
from jax.experimental.pallas import tpu as pltpu
from jax.sharding import Mesh
from jax.sharding import PartitionSpec as P

ROW = ("z", "y", "c")
CORES = 2
STEP = 4
PARAMS = pltpu.CompilerParams(vmem_limit_bytes=48 * 1024 * 1024)
SCALARS = pl.BlockSpec(memory_space=pltpu.SMEM)
ANYWHERE = pl.BlockSpec(memory_space=pl.ANY)


def dot32(a, b, dims=((1,), (0,))):
    return lax.dot_general(
        a, b, (dims, ((), ())), precision=lax.Precision.HIGHEST, preferred_element_type=jnp.float32
    )


def cut_kernel(pos_ref, w_ref, m_ref, b_ref, *o_refs):
    mb_ref, outs = o_refs[-1], o_refs[:-1]
    groups, cols = len(outs), outs[0].shape[2]
    lines = groups // CORES
    for k in range(groups):
        y = lax.rem(pos_ref[1] + k // CORES, lines)
        c = lax.rem(pos_ref[2] + k % CORES, CORES)
        at = pl.multiple_of((y * CORES + c) * cols, cols)
        outs[k][...] = w_ref[:, :, pl.ds(at, cols)]

    @pl.when(pl.program_id(0) == 0)
    def _():
        half = m_ref.shape[0]
        mb_ref[:half] = m_ref[...]
        mb_ref[half:] = b_ref[...]


def cut_by_owner(pos, weights, maps, basis, groups, planes):
    lay, rows, width = weights.shape
    cols = width // (groups * planes)
    both = (maps.shape[0] + basis.shape[0], maps.shape[1])
    spec = pltpu.PrefetchScalarGridSpec(
        num_scalar_prefetch=1,
        grid=(planes,),
        in_specs=[
            pl.BlockSpec(
                (lay, rows, groups * cols), lambda z, pos: (0, 0, lax.rem(pos[0] + z, planes))
            ),
            pl.BlockSpec(maps.shape, lambda z, pos: (0, 0)),
            pl.BlockSpec(basis.shape, lambda z, pos: (0, 0)),
        ],
        out_specs=[pl.BlockSpec((lay, rows, cols), lambda z, pos: (0, 0, z))] * groups
        + [pl.BlockSpec(both, lambda z, pos: (0, 0))],
    )
    *chunks, mine = pl.pallas_call(
        cut_kernel,
        grid_spec=spec,
        out_shape=[jax.ShapeDtypeStruct((lay, rows, planes * cols), weights.dtype)] * groups
        + [jax.ShapeDtypeStruct(both, weights.dtype)],
        compiler_params=PARAMS,
        name="cut_by_owner",
    )(pos, weights, maps, basis)
    return chunks, mine


def after_kernel(*refs):
    del refs


def after(first, arrays):
    return pl.pallas_call(
        after_kernel,
        in_specs=[ANYWHERE] * (len(arrays) + 1),
        out_specs=[ANYWHERE] * len(arrays),
        out_shape=[jax.ShapeDtypeStruct(a.shape, a.dtype) for a in arrays],
        input_output_aliases={i: i for i in range(len(arrays))},
        name="after",
    )(*arrays, first)


def residual_kernel(count, *refs):
    w_refs, (c_ref, d_ref, b_ref, m_ref) = refs[:count], refs[count : count + 4]
    *s_refs, acc_ref, all_ref = refs[-count - 2 :]
    r_ref = refs[-count - 3]
    step, _, cols = b_ref.shape
    rows = w_refs[0].shape[1]
    layer, plane = pl.program_id(0), pl.program_id(1)

    @pl.when((layer == 0) & (plane == 0))
    def _():
        acc_ref[...] = jnp.zeros_like(acc_ref)

    @pl.when(plane == 0)
    def _():
        for k in range(count):
            all_ref[k * rows : (k + 1) * rows] = (c_ref, d_ref)[k % CORES][k // CORES, 0]

    total = None
    for i in range(step):
        here = slice(i * cols, (i + 1) * cols)
        low = jnp.dot(all_ref[...], b_ref[i], preferred_element_type=jnp.float32)
        w = jnp.concatenate([w_ref[0, :, here] for w_ref in w_refs], axis=0)
        res = (w.astype(jnp.float32) - low).astype(jnp.bfloat16)
        r_ref[0, i] = res
        part = jnp.dot(res, m_ref[i], preferred_element_type=jnp.float32)
        total = part if total is None else total + part
    acc_ref[...] += total

    @pl.when((layer == pl.num_programs(0) - 1) & (plane == pl.num_programs(1) - 1))
    def _():
        for k in range(count):
            s_refs[k][...] = acc_ref[k * rows : (k + 1) * rows]


def residual_and_sketch(half, halves, chunks, near, others, maps_basis, before):
    count = len(chunks)
    lay, rows, width = chunks[0].shape
    planes, _, sw = maps_basis.shape
    rank = near.shape[3]
    cols = width // planes
    tall = count * rows
    coeff = pl.BlockSpec((count // CORES, 1, rows, rank), lambda l, z: (half, l, 0, 0))
    kept = [] if before is None else [before]
    return pl.pallas_call(
        functools.partial(residual_kernel, count),
        grid=(lay, planes // STEP),
        in_specs=[pl.BlockSpec((1, rows, cols * STEP), lambda l, z: (l, 0, z))] * count
        + [
            coeff,
            coeff,
            pl.BlockSpec((STEP, rank, cols), lambda l, z: (z, 1, 0)),
            pl.BlockSpec((STEP, cols, sw), lambda l, z: (z, l, 0)),
        ]
        + [ANYWHERE] * len(kept),
        out_specs=[pl.BlockSpec((1, STEP, tall, cols), lambda l, z: (l, z, half, 0))]
        + [pl.BlockSpec((rows, sw), lambda l, z: (0, 0))] * count,
        out_shape=[jax.ShapeDtypeStruct((lay, planes, halves * tall, cols), jnp.bfloat16)]
        + [jax.ShapeDtypeStruct((rows, sw), jnp.float32)] * count,
        input_output_aliases={count + 4: 0} if kept else {},
        scratch_shapes=[
            pltpu.VMEM((tall, sw), jnp.float32),
            pltpu.VMEM((tall, rank), jnp.bfloat16),
        ],
        compiler_params=PARAMS,
        name="residual_and_sketch",
    )(*chunks, near, others, maps_basis, maps_basis, *kept)


def gram_kernel(pos_ref, *refs):
    both_ref, g_ref, t_ref = refs[-3:]
    sketch = jnp.concatenate([ref[...] for ref in refs[:-3]], axis=0)
    half, sw = g_ref.shape
    t_ref[...] = sketch.T
    g_ref[...] = dot32(t_ref[pl.ds(pl.multiple_of(pos_ref[2] * half, half), half)], sketch)
    high = t_ref[...].astype(jnp.bfloat16)
    both_ref[:sw] = high
    both_ref[sw:] = (t_ref[...] - high.astype(jnp.float32)).astype(jnp.bfloat16)


def stack_and_gram(pos, parts):
    rows, sw = parts[0].shape
    tall = rows * len(parts)
    return pl.pallas_call(
        gram_kernel,
        in_specs=[SCALARS] + [pl.BlockSpec((rows, sw), lambda: (0, 0))] * len(parts),
        out_shape=[
            jax.ShapeDtypeStruct((2 * sw, tall), jnp.bfloat16),
            jax.ShapeDtypeStruct((sw // CORES, sw), jnp.float32),
        ],
        scratch_shapes=[pltpu.VMEM((sw, tall), jnp.float32)],
        compiler_params=PARAMS,
        name="stack_and_gram",
    )(pos, *parts)


def project_kernel(both_ref, *refs):
    ways = len(refs) // 2
    sw = both_ref.shape[0] // 2
    for i in range(ways):
        out = jnp.dot(both_ref[...], refs[i][0, 0], preferred_element_type=jnp.float32)
        refs[ways + i][0] = out[:sw] + out[sw:]


def project(both, residual, first, rounds):
    lay, planes, rows, cols = residual.shape
    sw = both.shape[0] // 2
    mid = planes // 2
    places = (
        lambda r: (0, mid - first - r, 0, 0),
        lambda r: (0, lax.rem(mid + 1 + first + r, planes), 0, 0),
        lambda r: (1, mid - 1 - first - r, 0, 0),
        lambda r: (1, mid + first + r, 0, 0),
    )
    return pl.pallas_call(
        project_kernel,
        grid=(rounds,),
        in_specs=[pl.BlockSpec(both.shape, lambda r: (0, 0))]
        + [pl.BlockSpec((1, 1, rows, cols), place) for place in places],
        out_specs=[pl.BlockSpec((1, sw, cols), lambda r: (r, 0, 0))] * len(places),
        out_shape=[jax.ShapeDtypeStruct((rounds, sw, cols), jnp.float32)] * len(places),
        compiler_params=PARAMS,
        name="project",
    )(both, *[residual] * len(places))


def factor_block(a):
    n = a.shape[0]
    row = lax.broadcasted_iota(jnp.int32, (n, n), 0)
    col = lax.broadcasted_iota(jnp.int32, (n, n), 1)
    both = jnp.concatenate([a, jnp.where(row == col, 1.0, 0.0)], axis=1)
    done = []
    for j in range(n):
        r = j % 8
        if j and r == 0:
            both = both[8:]
        pivot = lax.rsqrt(both[r : r + 1, j : j + 1])
        line = both[r : r + 1, :] * pivot
        mult = both[:, j : j + 1] * pivot
        done.append(line)
        if r < 7:
            keep = lax.broadcasted_iota(jnp.int32, (both.shape[0], 1), 0) > r
            mult = jnp.where(keep, mult, 0.0)
        both = both - mult * line
    return jnp.concatenate(done, axis=0)[:, n:]


def upper_kernel(pos_ref, mine_ref, other_ref, inv_ref, cross_ref, rest_ref):
    half = mine_ref.shape[0]
    first = pos_ref[2] == 0
    top = jnp.where(first, mine_ref[...], other_ref[...])
    low = jnp.where(first, other_ref[...], mine_ref[...])
    inv = factor_block(top[:, :half])
    panel = dot32(low[:, :half], inv, ((1,), (1,)))
    inv_ref[...] = inv
    cross_ref[...] = dot32(panel, inv)
    rest_ref[...] = low[:, half:] - dot32(panel, panel, ((1,), (1,)))


def upper_factor(pos, mine, other):
    half = mine.shape[0]
    return pl.pallas_call(
        upper_kernel,
        in_specs=[SCALARS] + [pl.BlockSpec(mine.shape, lambda: (0, 0))] * 2,
        out_shape=[jax.ShapeDtypeStruct((half, half), jnp.float32)] * 3,
        compiler_params=PARAMS,
        name="upper_factor",
    )(pos, mine, other)


def lower_kernel(inv_ref, cross_ref, rest_ref, o_ref):
    half = inv_ref.shape[0]
    inv = factor_block(rest_ref[...])
    o_ref[:half, :half] = inv_ref[...]
    o_ref[:half, half:] = jnp.zeros_like(inv)
    o_ref[half:, :half] = -dot32(inv, cross_ref[...])
    o_ref[half:, half:] = inv


def lower_factor(inv, cross, rest):
    full = 2 * inv.shape[0]
    return pl.pallas_call(
        lower_kernel,
        out_shape=jax.ShapeDtypeStruct((full, full), jnp.float32),
        compiler_params=PARAMS,
        name="lower_factor",
    )(inv, cross, rest)


def finish_kernel(ranks_ref, inv_ref, *refs):
    o_ref = refs[-1]
    for l in range(o_ref.shape[0]):
        own, up, down = refs[3 * l : 3 * l + 3]
        out = dot32(inv_ref[...], own[...].reshape(up.shape) + up[...] + down[...])
        kept = lax.broadcasted_iota(jnp.int32, out.shape, 0) < ranks_ref[l]
        o_ref[l] = jnp.where(kept, out, 0.0)


def finish(ranks, inv, shares):
    sw, cols = shares[0][1].shape
    flat = [x for share in shares for x in share]
    return pl.pallas_call(
        finish_kernel,
        in_specs=[SCALARS] + [pl.BlockSpec(memory_space=pltpu.VMEM)] * (1 + len(flat)),
        out_shape=jax.ShapeDtypeStruct((len(shares), sw, cols), jnp.float32),
        compiler_params=PARAMS,
        name="finish",
    )(ranks, inv, *flat)


def shift(x, axis, size, k):
    return lax.ppermute(x, axis, [(i, (i + k) % size) for i in range(size)])


def shift_group(x, groups, k, sign=1):
    lines = groups // CORES
    pairs = [
        (y * CORES + c, (y + sign * (k // CORES)) % lines * CORES + (c + k) % CORES)
        for y in range(lines)
        for c in range(CORES)
    ]
    return lax.ppermute(x, ("y", "c"), pairs)


def added(parts):
    return sum(parts[1:], parts[0])


def ring_gather(x, axis, size):
    got = {0: x}
    up = down = x
    for k in range(1, size // 2 + 1):
        up = shift(up, axis, size, -1)
        got[k] = up
        if k < size - k:
            down = shift(down, axis, size, 1)
            got[size - k] = down
    return jnp.stack([got[k] for k in range(size)])


def per_device(planes, groups, lines, weights, coeffs, basis, sketch_map, ranks):
    lay = weights.shape[0]
    sw = sketch_map.shape[2]
    ys = groups // CORES
    pos = jnp.stack([lax.axis_index(a) for a in ROW]).astype(jnp.int32)
    near = jnp.stack([coeffs] + [shift(coeffs, "y", ys, k) for k in range(1, ys)])
    others = shift(near, "c", CORES, 1)
    chunks, own = cut_by_owner(pos, weights, sketch_map.reshape(-1, sw), basis, groups, planes)
    chunks = after(near, chunks)
    chunks = [chunks[0]] + [shift_group(chunks[k], groups, k) for k in range(1, groups)]
    maps_basis = ring_gather(own, "z", planes)
    halves, residual, parts = 2, None, []
    count = groups // halves
    for half in range(halves):
        residual, *some = residual_and_sketch(
            half, halves, chunks[half * count :][:count], near, others, maps_basis, residual
        )
        parts += some
    mine = added([parts[0]] + [shift_group(parts[k], groups, k, -1) for k in range(1, groups)])
    mine = added([mine] + [shift(mine, "x", lines, k) for k in range(1, lines)])
    both, gram = stack_and_gram(pos, [mine] + [shift_group(mine, groups, k) for k in range(1, groups)])

    gram = gram + shift(gram, "z", planes, planes // 2)
    gram = added([gram] + [shift(gram, "z", planes, k) for k in (1, -1, 2)])
    inv = lower_factor(*upper_factor(pos, gram, shift(gram, "c", CORES, 1)))

    ways = (1, -1, 1, -1)
    sent = [p[0] for p in project(both, residual, 0, 1)]
    later = project(both, residual, 1, planes // 2 - 1)
    for r in range(planes // 2 - 1):
        sent = [shift(v, "z", planes, way) for v, way in zip(sent, ways)]
        for i in range(4):
            if r < planes // 2 - 2 or i in (0, 3):
                sent[i] = later[i][r] + sent[i]
    for i in (0, 3):
        sent[i] = shift(sent[i], "z", planes, ways[i])
    shares = [(later[1 + i][-1], sent[2 * i], sent[2 * i + 1]) for i in range(lay)]
    ranks_here = lax.dynamic_slice_in_dim(ranks, lax.axis_index("x") * lay, lay)
    return finish(ranks_here, inv, shares)


def solution(mesh):
    wide, lines = mesh.devices.shape
    groups = 8
    planes = wide // groups
    fine = Mesh(mesh.devices.reshape(planes, groups // CORES, CORES, lines), ROW + ("x",))
    in_specs = (
        P("x", ROW, None),
        P("x", ROW, None),
        P(None, ROW),
        P("x", ROW, None),
        P(),
    )
    return jax.shard_map(
        functools.partial(per_device, planes, groups, lines),
        mesh=fine,
        in_specs=in_specs,
        out_specs=P("x", None, ROW),
        check_vma=False,
    )
```

```python
import functools

import jax
import jax.numpy as jnp
from jax import lax
from jax.experimental import pallas as pl
from jax.experimental.pallas import tpu as pltpu
from jax.sharding import Mesh
from jax.sharding import PartitionSpec as P

ROW = ("z", "y", "c")
CORES = 2
STEP = 4
PARAMS = pltpu.CompilerParams(vmem_limit_bytes=48 * 1024 * 1024)
SCALARS = pl.BlockSpec(memory_space=pltpu.SMEM)
ANYWHERE = pl.BlockSpec(memory_space=pl.ANY)


def dot32(a, b, dims=((1,), (0,))):
    return lax.dot_general(
        a, b, (dims, ((), ())), precision=lax.Precision.HIGHEST, preferred_element_type=jnp.float32
    )


def cut_kernel(*refs):
    w_refs, o_ref = refs[1:-1], refs[-1]
    groups, cols = o_ref.shape[0], o_ref.shape[3] // len(w_refs)
    for i, w_ref in enumerate(w_refs):
        for g in range(groups):
            here = slice(g * cols, (g + 1) * cols)
            o_ref[g, :, :, i * cols : (i + 1) * cols] = w_ref[:, :, here]


def cut_by_owner(pos, weights, groups, planes):
    lay, rows, width = weights.shape
    cols = width // (groups * planes)
    ways = 2

    def place(i):
        return lambda z, pos: (0, 0, lax.rem(pos[0] + ways * z + i, planes))

    spec = pltpu.PrefetchScalarGridSpec(
        num_scalar_prefetch=1,
        grid=(planes // ways,),
        in_specs=[pl.BlockSpec((lay, rows, groups * cols), place(i)) for i in range(ways)],
        out_specs=pl.BlockSpec((groups, lay, rows, cols * ways), lambda z, pos: (0, 0, 0, z)),
    )
    return pl.pallas_call(
        cut_kernel,
        grid_spec=spec,
        out_shape=pltpu.HBM((groups, lay, rows, planes * cols), weights.dtype),
        compiler_params=PARAMS,
        name="cut_by_owner",
    )(pos, *[weights] * ways)


def after_kernel(*refs):
    del refs


def after(first, arrays):
    return pl.pallas_call(
        after_kernel,
        in_specs=[ANYWHERE] * (len(arrays) + 1),
        out_specs=[ANYWHERE] * len(arrays),
        out_shape=[pltpu.HBM(a.shape, a.dtype) for a in arrays],
        input_output_aliases={i: i for i in range(len(arrays))},
        name="after",
    )(*arrays, first)


def group_back(pos_ref, k, groups):
    lines = groups // CORES
    y = lax.rem(pos_ref[1] - k // CORES + lines, lines)
    c = lax.rem(pos_ref[2] + k % CORES, CORES)
    return y * CORES + c


def residual_kernel(count, _, *refs):
    w_refs, (c_ref, d_ref, b_ref, m_ref) = refs[:count], refs[count : count + 4]
    r_ref, keep_ref, send_ref, acc_ref, all_ref = refs[-5:]
    step, _, cols = b_ref.shape
    rows = w_refs[0].shape[2]
    layer, plane = pl.program_id(0), pl.program_id(1)

    @pl.when((layer == 0) & (plane == 0))
    def _():
        acc_ref[...] = jnp.zeros_like(acc_ref)

    @pl.when(plane == 0)
    def _():
        for k in range(count):
            all_ref[k * rows : (k + 1) * rows] = (c_ref, d_ref)[k % CORES][k // CORES, 0]

    total = None
    for i in range(step):
        here = slice(i * cols, (i + 1) * cols)
        low = jnp.dot(all_ref[...], b_ref[i], preferred_element_type=jnp.float32)
        w = jnp.concatenate([w_ref[0, 0, :, here] for w_ref in w_refs], axis=0)
        res = (w.astype(jnp.float32) - low).astype(jnp.bfloat16)
        r_ref[0, i] = res
        part = jnp.dot(res, m_ref[i, 0], preferred_element_type=jnp.float32)
        total = part if total is None else total + part
    acc_ref[...] += total

    @pl.when((layer == pl.num_programs(0) - 1) & (plane == pl.num_programs(1) - 1))
    def _():
        for k in range(count):
            (keep_ref, send_ref)[k % CORES][k // CORES] = acc_ref[k * rows : (k + 1) * rows]


def residual_and_sketch(pos, half, halves, w, near, others, maps, basis, before):
    groups, lay, rows, width = w.shape
    count = groups // halves
    planes, _, _, sw = maps.shape
    rank = near.shape[3]
    cols = width // planes
    tall = count * rows
    coeff = pl.BlockSpec((count // CORES, 1, rows, rank), lambda l, z, pos: (half, l, 0, 0))
    kept = [] if before is None else [before]

    def place(k):
        return lambda l, z, pos: (group_back(pos, half * count + k, groups), l, 0, z)

    spec = pltpu.PrefetchScalarGridSpec(
        num_scalar_prefetch=1,
        grid=(lay, planes // STEP),
        in_specs=[pl.BlockSpec((1, 1, rows, cols * STEP), place(k)) for k in range(count)]
        + [
            coeff,
            coeff,
            pl.BlockSpec((STEP, rank, cols), lambda l, z, pos: (z, 0, 0)),
            pl.BlockSpec((STEP, 1, cols, sw), lambda l, z, pos: (z, l, 0, 0)),
        ]
        + [ANYWHERE] * len(kept),
        out_specs=[pl.BlockSpec((1, STEP, tall, cols), lambda l, z, pos: (l, z, half, 0))]
        + [pl.BlockSpec((count // CORES, rows, sw), lambda l, z, pos: (0, 0, 0))] * CORES,
        scratch_shapes=[
            pltpu.VMEM((tall, sw), jnp.float32),
            pltpu.VMEM((tall, rank), jnp.bfloat16),
        ],
    )
    return pl.pallas_call(
        functools.partial(residual_kernel, count),
        grid_spec=spec,
        out_shape=[jax.ShapeDtypeStruct((lay, planes, halves * tall, cols), jnp.bfloat16)]
        + [jax.ShapeDtypeStruct((count // CORES, rows, sw), jnp.float32)] * CORES,
        input_output_aliases={count + 5: 0} if kept else {},
        compiler_params=PARAMS,
        name="residual_and_sketch",
    )(pos, *[w] * count, near, others, basis, maps, *kept)


def gram_kernel(pos_ref, near_ref, other_ref, both_ref, g_ref, t_ref):
    ys = near_ref.shape[0]
    sketch = [ref[k] for k in range(ys) for ref in (near_ref, other_ref)]
    sketch = jnp.concatenate(sketch, axis=0)
    share, sw = g_ref.shape
    t_ref[...] = sketch.T
    at = pl.multiple_of((pos_ref[3] * CORES + pos_ref[2]) * share, share)
    g_ref[...] = dot32(t_ref[pl.ds(at, share)], sketch)
    high = t_ref[...].astype(jnp.bfloat16)
    both_ref[:sw] = high
    both_ref[sw:] = (t_ref[...] - high.astype(jnp.float32)).astype(jnp.bfloat16)


def stack_and_gram(pos, near, others, lines):
    ys, rows, sw = near.shape
    tall = rows * ys * CORES
    return pl.pallas_call(
        gram_kernel,
        in_specs=[SCALARS] + [pl.BlockSpec(near.shape, lambda: (0, 0, 0))] * CORES,
        out_shape=[
            jax.ShapeDtypeStruct((2 * sw, tall), jnp.bfloat16),
            jax.ShapeDtypeStruct((sw // (CORES * lines), sw), jnp.float32),
        ],
        scratch_shapes=[pltpu.VMEM((sw, tall), jnp.float32)],
        compiler_params=PARAMS,
        name="stack_and_gram",
    )(pos, near, others)


def project_kernel(both_ref, *refs):
    r_refs, o_refs = refs[:4], refs[4:]
    sw = both_ref.shape[0] // 2
    for i, r_ref in enumerate(r_refs):
        out = jnp.dot(both_ref[...], r_ref[0, 0], preferred_element_type=jnp.float32)
        o_refs[i % 2][0, i // 2] = out[:sw] + out[sw:]


def project(both, residual, first, rounds):
    lay, planes, rows, cols = residual.shape
    sw = both.shape[0] // 2
    mid = planes // 2
    places = (
        lambda r: (0, mid - first - r, 0, 0),
        lambda r: (0, lax.rem(mid + 1 + first + r, planes), 0, 0),
        lambda r: (1, mid - 1 - first - r, 0, 0),
        lambda r: (1, mid + first + r, 0, 0),
    )
    return pl.pallas_call(
        project_kernel,
        grid=(rounds,),
        in_specs=[pl.BlockSpec(both.shape, lambda r: (0, 0))]
        + [pl.BlockSpec((1, 1, rows, cols), place) for place in places],
        out_specs=[pl.BlockSpec((1, lay, sw, cols), lambda r: (r, 0, 0, 0))] * 2,
        out_shape=[jax.ShapeDtypeStruct((rounds, lay, sw, cols), jnp.float32)] * 2,
        compiler_params=PARAMS,
        name="project",
    )(both, *[residual] * len(places))


def factor_block(a):
    n = a.shape[0]
    row = lax.broadcasted_iota(jnp.int32, (n, n), 0)
    col = lax.broadcasted_iota(jnp.int32, (n, n), 1)
    both = jnp.concatenate([a, jnp.where(row == col, 1.0, 0.0)], axis=1)
    done = []
    for j in range(n):
        r = j % 8
        if j and r == 0:
            both = both[8:]
        pivot = lax.rsqrt(both[r : r + 1, j : j + 1])
        line = both[r : r + 1, :] * pivot
        mult = both[:, j : j + 1] * pivot
        done.append(line)
        if r < 7:
            keep = lax.broadcasted_iota(jnp.int32, (both.shape[0], 1), 0) > r
            mult = jnp.where(keep, mult, 0.0)
        both = both - mult * line
    return jnp.concatenate(done, axis=0)[:, n:]


def upper_kernel(pos_ref, mine_ref, other_ref, *refs):
    inv_ref, cross_ref, rest_ref, g_ref = refs[-4:]
    lines, share, _ = mine_ref.shape
    half = inv_ref.shape[0]
    for k in range(lines):
        x = lax.rem(pos_ref[3] - k + lines, lines) * CORES
        for c, ref in ((pos_ref[2], mine_ref), (1 - pos_ref[2], other_ref)):
            g_ref[pl.ds(pl.multiple_of((x + c) * share, share), share)] = ref[k]
    inv = factor_block(g_ref[:half, :half])
    panel = dot32(g_ref[half:, :half], inv, ((1,), (1,)))
    inv_ref[...] = inv
    cross_ref[...] = dot32(panel, inv)
    rest_ref[...] = g_ref[half:, half:] - dot32(panel, panel, ((1,), (1,)))


def upper_factor(pos, mine, other, first):
    lines, share, sw = mine.shape
    half = sw // 2
    return pl.pallas_call(
        upper_kernel,
        in_specs=[SCALARS]
        + [pl.BlockSpec(mine.shape, lambda: (0, 0, 0))] * 2
        + [ANYWHERE] * len(first),
        out_shape=[jax.ShapeDtypeStruct((half, half), jnp.float32)] * 3,
        scratch_shapes=[pltpu.VMEM((sw, sw), jnp.float32)],
        compiler_params=PARAMS,
        name="upper_factor",
    )(pos, mine, other, *first)


def lower_kernel(inv_ref, cross_ref, rest_ref, *refs):
    o_ref = refs[-1]
    half = inv_ref.shape[0]
    inv = factor_block(rest_ref[...])
    o_ref[:half, :half] = inv_ref[...]
    o_ref[:half, half:] = jnp.zeros_like(inv)
    o_ref[half:, :half] = -dot32(inv, cross_ref[...])
    o_ref[half:, half:] = inv


def lower_factor(inv, cross, rest, first):
    full = 2 * inv.shape[0]
    return pl.pallas_call(
        lower_kernel,
        in_specs=[pl.BlockSpec(inv.shape, lambda: (0, 0))] * 3 + [ANYWHERE] * len(first),
        out_shape=jax.ShapeDtypeStruct((full, full), jnp.float32),
        compiler_params=PARAMS,
        name="lower_factor",
    )(inv, cross, rest, *first)


def add_kernel(*refs):
    refs[-2][...] = refs[0][0] + refs[2][...]
    refs[-1][...] = refs[1][0] + refs[3][...]


def ring_add(later, got, r, first):
    rounds, lay, sw, cols = later[0].shape
    one = r == rounds - 1
    n = 1 if one else lay
    where = (0, 1) if one else (0, 0)
    return pl.pallas_call(
        add_kernel,
        grid=(1,),
        in_specs=[pl.BlockSpec((1, n, sw, cols), lambda i, w=w: (r, w, 0, 0)) for w in where]
        + [pl.BlockSpec((n, sw, cols), lambda i, w=w: (w, 0, 0)) for w in where]
        + [ANYWHERE] * len(first),
        out_specs=[pl.BlockSpec((n, sw, cols), lambda i: (0, 0, 0))] * 2,
        out_shape=[jax.ShapeDtypeStruct((n, sw, cols), jnp.float32)] * 2,
        compiler_params=PARAMS,
        name="ring_add",
    )(*later, *got, *first)


def finish_kernel(ranks_ref, inv_ref, up_own, down_own, up_got, down_got, up_last, down_last, o_ref):
    sums = (
        down_own[0, 0] + down_got[0] + up_last[0],
        up_own[0, 0] + up_got[0] + down_last[0],
    )
    for l, total in enumerate(sums):
        out = dot32(inv_ref[...], total)
        kept = lax.broadcasted_iota(jnp.int32, out.shape, 0) < ranks_ref[l]
        o_ref[l] = jnp.where(kept, out, 0.0)


def finish(ranks, inv, later, got, last):
    rounds, lay, sw, cols = later[0].shape
    end = rounds - 1
    return pl.pallas_call(
        finish_kernel,
        grid=(1,),
        in_specs=[
            SCALARS,
            pl.BlockSpec((sw, sw), lambda i: (0, 0)),
            pl.BlockSpec((1, 1, sw, cols), lambda i: (end, 1, 0, 0)),
            pl.BlockSpec((1, 1, sw, cols), lambda i: (end, 0, 0, 0)),
            pl.BlockSpec((1, sw, cols), lambda i: (1, 0, 0)),
            pl.BlockSpec((1, sw, cols), lambda i: (0, 0, 0)),
            pl.BlockSpec((1, sw, cols), lambda i: (0, 0, 0)),
            pl.BlockSpec((1, sw, cols), lambda i: (0, 0, 0)),
        ],
        out_specs=pl.BlockSpec((lay, sw, cols), lambda i: (0, 0, 0)),
        out_shape=jax.ShapeDtypeStruct((lay, sw, cols), jnp.float32),
        compiler_params=PARAMS,
        name="finish",
    )(ranks, inv, *later, *got, *last)


def shift(x, axis, size, k):
    return lax.ppermute(x, axis, [(i, (i + k) % size) for i in range(size)])


def added(parts):
    return sum(parts[1:], parts[0])


def ring_gather(arrays, axis, size):
    got = [{0: x} for x in arrays]
    up, down = list(arrays), list(arrays)
    for k in range(1, size // 2 + 1):
        for i in range(len(arrays)):
            got[i][k] = up[i] = shift(up[i], axis, size, -1)
            if k < size - k:
                got[i][size - k] = down[i] = shift(down[i], axis, size, 1)
    return [jnp.stack([g[k] for k in range(size)]) for g in got]


def per_device(planes, groups, lines, weights, coeffs, basis, sketch_map, ranks):
    lay = weights.shape[0]
    ys = groups // CORES
    pos = jnp.stack([lax.axis_index(a) for a in (*ROW, "x")]).astype(jnp.int32)
    near = jnp.stack([coeffs] + [shift(coeffs, "y", ys, k) for k in range(1, ys)])
    all_maps, all_basis = ring_gather((sketch_map, basis), "z", planes)
    (cut,) = after(near, [cut_by_owner(pos, weights, groups, planes)])
    others = shift(near, "c", CORES, 1)
    w = lax.all_to_all(cut, ("y", "c"), 0, 0, tiled=True)
    halves, residual, parts = 2, None, []
    for half in range(halves):
        residual, keep, send = residual_and_sketch(
            pos, half, halves, w, near, others, all_maps, all_basis, residual
        )
        got = shift(send, "c", CORES, 1)
        parts += [keep[i] + got[i] for i in range(ys // halves)]
    mine = added([parts[0]] + [shift(parts[k], "y", ys, -k) for k in range(1, ys)])
    mine = added([mine] + [shift(mine, "x", lines, k) for k in range(1, lines)])
    rows_near = jnp.stack([mine] + [shift(mine, "y", ys, k) for k in range(1, ys)])
    both, gram = stack_and_gram(pos, rows_near, shift(rows_near, "c", CORES, 1), lines)

    gram = gram + shift(gram, "z", planes, planes // 2)
    sent = [p[0] for p in project(both, residual, 0, 1)]
    later = project(both, residual, 1, planes // 2 - 1)
    gram = added([gram] + [shift(gram, "z", planes, k) for k in (1, -1, 2)])
    gram = jnp.stack([gram] + [shift(gram, "x", lines, k) for k in range(1, lines)])
    other = shift(gram, "c", CORES, 1)

    def send_both(pair):
        return shift(pair[0], "z", planes, 1), shift(pair[1], "z", planes, -1)

    sent = ring_add(later, send_both(sent), 0, [other])
    upper = upper_factor(pos, gram, other, sent)
    sent = ring_add(later, send_both(sent), 1, upper[:1])
    inv = lower_factor(*upper, sent)
    got = send_both(sent)
    last = send_both(ring_add(later, got, 2, [inv]))
    ranks_here = lax.dynamic_slice_in_dim(ranks, lax.axis_index("x") * lay, lay)
    return finish(ranks_here, inv, later, got, last)


def solution(mesh):
    wide, lines = mesh.devices.shape
    groups = 8
    planes = wide // groups
    fine = Mesh(mesh.devices.reshape(planes, groups // CORES, CORES, lines), ROW + ("x",))
    in_specs = (
        P("x", ROW, None),
        P("x", ROW, None),
        P(None, ROW),
        P("x", ROW, None),
        P(),
    )
    return jax.shard_map(
        functools.partial(per_device, planes, groups, lines),
        mesh=fine,
        in_specs=in_specs,
        out_specs=P("x", None, ROW),
        check_vma=False,
    )
```

```python
import functools

import jax
import jax.numpy as jnp
from jax import lax
from jax.experimental import pallas as pl
from jax.experimental.pallas import tpu as pltpu
from jax.sharding import Mesh
from jax.sharding import PartitionSpec as P

ROW = ("z", "y", "c")
CORES = 2
STEP = 4
SMALL = pltpu.CompilerParams(vmem_limit_bytes=8 * 1024 * 1024)
LARGE = pltpu.CompilerParams(vmem_limit_bytes=24 * 1024 * 1024)
SCALARS = pl.BlockSpec(memory_space=pltpu.SMEM)
ANYWHERE = pl.BlockSpec(memory_space=pl.ANY)


def dot32(a, b, dims=((1,), (0,))):
    return lax.dot_general(
        a, b, (dims, ((), ())), precision=lax.Precision.HIGHEST, preferred_element_type=jnp.float32
    )


def cut_kernel(*refs):
    w_refs, o_ref = refs[1:-1], refs[-1]
    groups, cols = o_ref.shape[0], o_ref.shape[3] // len(w_refs)
    for i, w_ref in enumerate(w_refs):
        for g in range(groups):
            here = slice(g * cols, (g + 1) * cols)
            o_ref[g, :, :, i * cols : (i + 1) * cols] = w_ref[:, :, here]


def cut_by_owner(pos, weights, groups, planes):
    lay, rows, width = weights.shape
    cols = width // (groups * planes)
    ways = 2

    def place(i):
        return lambda z, pos: (0, 0, lax.rem(pos[0] + ways * z + i, planes))

    spec = pltpu.PrefetchScalarGridSpec(
        num_scalar_prefetch=1,
        grid=(planes // ways,),
        in_specs=[pl.BlockSpec((lay, rows, groups * cols), place(i)) for i in range(ways)],
        out_specs=pl.BlockSpec((groups, lay, rows, cols * ways), lambda z, pos: (0, 0, 0, z)),
    )
    return pl.pallas_call(
        cut_kernel,
        grid_spec=spec,
        out_shape=pltpu.HBM((groups, lay, rows, planes * cols), weights.dtype),
        compiler_params=LARGE,
        name="cut_by_owner",
    )(pos, *[weights] * ways)


def after_kernel(*refs):
    del refs


def after(first, arrays):
    return pl.pallas_call(
        after_kernel,
        in_specs=[ANYWHERE] * (len(arrays) + len(first)),
        out_specs=[ANYWHERE] * len(arrays),
        out_shape=[pltpu.HBM(a.shape, a.dtype) for a in arrays],
        input_output_aliases={i: i for i in range(len(arrays))},
        name="after",
    )(*arrays, *first)


def group_back(pos_ref, k, groups):
    lines = groups // CORES
    y = lax.rem(pos_ref[1] - k // CORES + lines, lines)
    c = lax.rem(pos_ref[2] + k % CORES, CORES)
    return y * CORES + c


def residual_kernel(count, _, *refs):
    w_refs, (c_ref, d_ref, b_ref, m_ref) = refs[:count], refs[count : count + 4]
    r_ref, keep_ref, send_ref, acc_ref, all_ref = refs[-5:]
    step, _, cols = b_ref.shape
    rows = w_refs[0].shape[2]
    layer, plane = pl.program_id(0), pl.program_id(1)

    @pl.when((layer == 0) & (plane == 0))
    def _():
        acc_ref[...] = jnp.zeros_like(acc_ref)

    @pl.when(plane == 0)
    def _():
        for k in range(count):
            all_ref[k * rows : (k + 1) * rows] = (c_ref, d_ref)[k % CORES][k // CORES, 0]

    total = None
    for i in range(step):
        here = slice(i * cols, (i + 1) * cols)
        low = jnp.dot(all_ref[...], b_ref[i], preferred_element_type=jnp.float32)
        w = jnp.concatenate([w_ref[0, 0, :, here] for w_ref in w_refs], axis=0)
        res = (w.astype(jnp.float32) - low).astype(jnp.bfloat16)
        r_ref[0, i] = res
        part = jnp.dot(res, m_ref[i, 0], preferred_element_type=jnp.float32)
        total = part if total is None else total + part
    acc_ref[...] += total

    @pl.when((layer == pl.num_programs(0) - 1) & (plane == pl.num_programs(1) - 1))
    def _():
        for k in range(count):
            (keep_ref, send_ref)[k % CORES][k // CORES] = acc_ref[k * rows : (k + 1) * rows]


def residual_and_sketch(pos, half, halves, w, near, others, maps, basis, before):
    groups, lay, rows, width = w.shape
    count = groups // halves
    planes, _, _, sw = maps.shape
    rank = near.shape[3]
    cols = width // planes
    tall = count * rows
    coeff = pl.BlockSpec((count // CORES, 1, rows, rank), lambda l, z, pos: (half, l, 0, 0))
    kept = [] if before is None else [before]

    def place(k):
        return lambda l, z, pos: (group_back(pos, half * count + k, groups), l, 0, z)

    spec = pltpu.PrefetchScalarGridSpec(
        num_scalar_prefetch=1,
        grid=(lay, planes // STEP),
        in_specs=[pl.BlockSpec((1, 1, rows, cols * STEP), place(k)) for k in range(count)]
        + [
            coeff,
            coeff,
            pl.BlockSpec((STEP, rank, cols), lambda l, z, pos: (z, 0, 0)),
            pl.BlockSpec((STEP, 1, cols, sw), lambda l, z, pos: (z, l, 0, 0)),
        ]
        + [ANYWHERE] * len(kept),
        out_specs=[pl.BlockSpec((1, STEP, tall, cols), lambda l, z, pos: (l, z, half, 0))]
        + [pl.BlockSpec((count // CORES, rows, sw), lambda l, z, pos: (0, 0, 0))] * CORES,
        scratch_shapes=[
            pltpu.VMEM((tall, sw), jnp.float32),
            pltpu.VMEM((tall, rank), jnp.bfloat16),
        ],
    )
    return pl.pallas_call(
        functools.partial(residual_kernel, count),
        grid_spec=spec,
        out_shape=[jax.ShapeDtypeStruct((lay, planes, halves * tall, cols), jnp.bfloat16)]
        + [jax.ShapeDtypeStruct((count // CORES, rows, sw), jnp.float32)] * CORES,
        input_output_aliases={count + 5: 0} if kept else {},
        compiler_params=LARGE,
        name="residual_and_sketch",
    )(pos, *[w] * count, near, others, basis, maps, *kept)


def gram_kernel(pos_ref, near_ref, other_ref, both_ref, g_ref, t_ref):
    ys = near_ref.shape[0]
    sketch = [ref[k] for k in range(ys) for ref in (near_ref, other_ref)]
    sketch = jnp.concatenate(sketch, axis=0)
    share, sw = g_ref.shape
    t_ref[...] = sketch.T
    at = pl.multiple_of((pos_ref[3] * CORES + pos_ref[2]) * share, share)
    g_ref[...] = dot32(t_ref[pl.ds(at, share)], sketch)
    high = t_ref[...].astype(jnp.bfloat16)
    both_ref[:sw] = high
    both_ref[sw:] = (t_ref[...] - high.astype(jnp.float32)).astype(jnp.bfloat16)


def stack_and_gram(pos, near, others, lines):
    ys, rows, sw = near.shape
    tall = rows * ys * CORES
    return pl.pallas_call(
        gram_kernel,
        in_specs=[SCALARS] + [pl.BlockSpec(near.shape, lambda: (0, 0, 0))] * CORES,
        out_shape=[
            jax.ShapeDtypeStruct((2 * sw, tall), jnp.bfloat16),
            jax.ShapeDtypeStruct((sw // (CORES * lines), sw), jnp.float32),
        ],
        scratch_shapes=[pltpu.VMEM((sw, tall), jnp.float32)],
        compiler_params=SMALL,
        name="stack_and_gram",
    )(pos, near, others)


def project_kernel(both_ref, *refs):
    r_refs, o_refs = refs[:4], refs[4:]
    sw = both_ref.shape[0] // 2
    for i, r_ref in enumerate(r_refs):
        out = jnp.dot(both_ref[...], r_ref[0, 0], preferred_element_type=jnp.float32)
        o_refs[i % 2][i // 2] = out[:sw] + out[sw:]


def project(both, residual, first, rounds):
    lay, planes, rows, cols = residual.shape
    sw = both.shape[0] // 2
    mid = planes // 2
    places = (
        lambda r: (0, mid - first - r, 0, 0),
        lambda r: (0, lax.rem(mid + 1 + first + r, planes), 0, 0),
        lambda r: (1, mid - 1 - first - r, 0, 0),
        lambda r: (1, mid + first + r, 0, 0),
    )
    return pl.pallas_call(
        project_kernel,
        grid=(rounds,),
        in_specs=[pl.BlockSpec(both.shape, lambda r: (0, 0))]
        + [pl.BlockSpec((1, 1, rows, cols), place) for place in places],
        out_specs=[pl.BlockSpec((lay, sw, cols), lambda r: (r, 0, 0))] * 2,
        out_shape=[jax.ShapeDtypeStruct((rounds * lay, sw, cols), jnp.float32)] * 2,
        compiler_params=LARGE,
        name="project",
    )(both, *[residual] * len(places))


def factor_block(a):
    n = a.shape[0]
    four = 4
    row = lax.broadcasted_iota(jnp.int32, (n, n), 0)
    col = lax.broadcasted_iota(jnp.int32, (n, n), 1)
    left, right = a, jnp.where(row == col, 1.0, 0.0)
    done = []
    for j in range(0, n, four):
        r = j % 8
        if j and r == 0:
            left, right = left[8:], right[8:]
        mults = [
            jnp.broadcast_to(left[:, j + k : j + k + 1], left.shape) for k in range(four)
        ]
        lines = []
        for k in range(four):
            here = slice(r + k, r + k + 1)
            lower, upper = left[here], right[here]
            mult = mults[k]
            for m, (done_left, done_right) in enumerate(lines):
                weight = mults[m][here]
                lower = lower - weight * done_left
                upper = upper - weight * done_right
                mult = mult - mults[m] * mults[m][here]
            pivot = lax.rsqrt(mult[here])
            mults[k] = mult * pivot
            lines.append((lower * pivot, upper * pivot))
        for k in range(four):
            left = left - mults[k] * lines[k][0]
            right = right - mults[k] * lines[k][1]
            done.append(lines[k][1])
    return jnp.concatenate(done, axis=0)


def upper_kernel(pos_ref, mine_ref, other_ref, *refs):
    inv_ref, cross_ref, rest_ref, g_ref = refs[-4:]
    lines, share, _ = mine_ref.shape
    half = inv_ref.shape[0]
    for k in range(lines):
        x = lax.rem(pos_ref[3] - k + lines, lines) * CORES
        for c, ref in ((pos_ref[2], mine_ref), (1 - pos_ref[2], other_ref)):
            g_ref[pl.ds(pl.multiple_of((x + c) * share, share), share)] = ref[k]
    inv = factor_block(g_ref[:half, :half])
    panel = dot32(g_ref[half:, :half], inv, ((1,), (1,)))
    inv_ref[...] = inv
    cross_ref[...] = dot32(panel, inv)
    rest_ref[...] = g_ref[half:, half:] - dot32(panel, panel, ((1,), (1,)))


def upper_factor(pos, mine, other, first):
    lines, share, sw = mine.shape
    half = sw // 2
    return pl.pallas_call(
        upper_kernel,
        in_specs=[SCALARS]
        + [pl.BlockSpec(mine.shape, lambda: (0, 0, 0))] * 2
        + [ANYWHERE] * len(first),
        out_shape=[jax.ShapeDtypeStruct((half, half), jnp.float32)] * 3,
        scratch_shapes=[pltpu.VMEM((sw, sw), jnp.float32)],
        compiler_params=SMALL,
        name="upper_factor",
    )(pos, mine, other, *first)


def lower_kernel(inv_ref, cross_ref, rest_ref, *refs):
    o_ref = refs[-1]
    half = inv_ref.shape[0]
    inv = factor_block(rest_ref[...])
    o_ref[:half, :half] = inv_ref[...]
    o_ref[:half, half:] = jnp.zeros_like(inv)
    o_ref[half:, :half] = -dot32(inv, cross_ref[...])
    o_ref[half:, half:] = inv


def lower_factor(inv, cross, rest, first):
    full = 2 * inv.shape[0]
    return pl.pallas_call(
        lower_kernel,
        in_specs=[pl.BlockSpec(inv.shape, lambda: (0, 0))] * 3 + [ANYWHERE] * len(first),
        out_shape=jax.ShapeDtypeStruct((full, full), jnp.float32),
        compiler_params=SMALL,
        name="lower_factor",
    )(inv, cross, rest, *first)


def sum_kernel(*refs):
    refs[-1][...] = refs[0][...] + refs[1][...]


def add_after(a, b, first):
    whole = pl.BlockSpec(a.shape, lambda: (0, 0))
    return pl.pallas_call(
        sum_kernel,
        in_specs=[whole] * 2 + [ANYWHERE] * len(first),
        out_specs=whole,
        out_shape=jax.ShapeDtypeStruct(a.shape, a.dtype),
        compiler_params=SMALL,
        name="add_after",
    )(a, b, *first)


def add_kernel(*refs):
    refs[-2][...] = refs[0][...] + refs[2][...]
    refs[-1][...] = refs[1][...] + refs[3][...]


def ring_add(later, got, r, first):
    rounds, (lay, sw, cols) = later[0].shape[0] // got[0].shape[0], got[0].shape
    one = r == rounds - 1
    n = 1 if one else lay
    where = (0, 1) if one else (0, 0)
    return pl.pallas_call(
        add_kernel,
        grid=(1,),
        in_specs=[pl.BlockSpec((n, sw, cols), lambda i, w=w: (lay // n * r + w, 0, 0)) for w in where]
        + [pl.BlockSpec((n, sw, cols), lambda i, w=w: (w, 0, 0)) for w in where]
        + [ANYWHERE] * len(first),
        out_specs=[pl.BlockSpec((n, sw, cols), lambda i: (0, 0, 0))] * 2,
        out_shape=[jax.ShapeDtypeStruct((n, sw, cols), jnp.float32)] * 2,
        compiler_params=SMALL,
        name="ring_add",
    )(*later, *got, *first)


def finish_kernel(ranks_ref, inv_ref, up_own, down_own, up_got, down_got, up_last, down_last, o_ref):
    sums = (
        down_own[0] + down_got[0] + up_last[0],
        up_own[0] + up_got[0] + down_last[0],
    )
    for l, total in enumerate(sums):
        out = dot32(inv_ref[...], total)
        kept = lax.broadcasted_iota(jnp.int32, out.shape, 0) < ranks_ref[l]
        o_ref[l] = jnp.where(kept, out, 0.0)


def finish(ranks, inv, later, got, last):
    lay, sw, cols = got[0].shape
    end = later[0].shape[0] - lay
    return pl.pallas_call(
        finish_kernel,
        grid=(1,),
        in_specs=[
            SCALARS,
            pl.BlockSpec((sw, sw), lambda i: (0, 0)),
            pl.BlockSpec((1, sw, cols), lambda i: (end + 1, 0, 0)),
            pl.BlockSpec((1, sw, cols), lambda i: (end, 0, 0)),
            pl.BlockSpec((1, sw, cols), lambda i: (1, 0, 0)),
            pl.BlockSpec((1, sw, cols), lambda i: (0, 0, 0)),
            pl.BlockSpec((1, sw, cols), lambda i: (0, 0, 0)),
            pl.BlockSpec((1, sw, cols), lambda i: (0, 0, 0)),
        ],
        out_specs=pl.BlockSpec((lay, sw, cols), lambda i: (0, 0, 0)),
        out_shape=jax.ShapeDtypeStruct((lay, sw, cols), jnp.float32),
        compiler_params=SMALL,
        name="finish",
    )(ranks, inv, *later, *got, *last)


def shift(x, axis, size, k):
    return lax.ppermute(x, axis, [(i, (i + k) % size) for i in range(size)])


def added(parts):
    return sum(parts[1:], parts[0])


def ring_gather(arrays, axis, size):
    got = [{0: x} for x in arrays]
    up, down = list(arrays), list(arrays)
    for k in range(1, size // 2 + 1):
        for i in range(len(arrays)):
            got[i][k] = up[i] = shift(up[i], axis, size, -1)
            if k < size - k:
                got[i][size - k] = down[i] = shift(down[i], axis, size, 1)
    return [jnp.stack([g[k] for k in range(size)]) for g in got]


def per_device(planes, groups, lines, weights, coeffs, basis, sketch_map, ranks):
    lay = weights.shape[0]
    ys = groups // CORES
    pos = jnp.stack([lax.axis_index(a) for a in (*ROW, "x")]).astype(jnp.int32)
    near = jnp.stack([coeffs] + [shift(coeffs, "y", ys, k) for k in range(1, ys)])
    all_maps, all_basis = ring_gather((sketch_map, basis), "z", planes)
    weights = pltpu.with_memory_space_constraint(weights, pltpu.HBM)
    (cut,) = after([near], [cut_by_owner(pos, weights, groups, planes)])
    others = shift(near, "c", CORES, 1)
    w = lax.all_to_all(cut, ("y", "c"), 0, 0, tiled=True)
    halves, residual, parts = 1, None, []
    for half in range(halves):
        residual, keep, send = residual_and_sketch(
            pos, half, halves, w, near, others, all_maps, all_basis, residual
        )
        got = shift(send, "c", CORES, 1)
        parts += [keep[i] + got[i] for i in range(ys // halves)]
    mine = added([parts[0]] + [shift(parts[k], "y", ys, -k) for k in range(1, ys)])
    mine = added([mine] + [shift(mine, "x", lines, k) for k in range(1, lines)])
    rows_near = jnp.stack([mine] + [shift(mine, "y", ys, k) for k in range(1, ys)])
    both, gram = stack_and_gram(pos, rows_near, shift(rows_near, "c", CORES, 1), lines)

    across = shift(gram, "z", planes, planes // 2)
    start = project(both, residual, 0, 1)
    later = project(both, residual, 1, planes // 2 - 1)
    gram = add_after(gram, across, start)
    start = after([gram], start)
    gram = added([gram] + [shift(gram, "z", planes, k) for k in (1, -1, 2)])
    gram = jnp.stack([gram] + [shift(gram, "x", lines, k) for k in range(1, lines)])
    other = shift(gram, "c", CORES, 1)

    def send_both(pair):
        return shift(pair[0], "z", planes, 1), shift(pair[1], "z", planes, -1)

    sent = ring_add(later, send_both(start), 0, [])
    got = send_both(sent)
    upper = upper_factor(pos, gram, other, sent)
    sent = ring_add(later, got, 1, upper[:1])
    got = send_both(sent)
    inv = lower_factor(*upper, sent)
    last = send_both(ring_add(later, got, 2, [inv]))
    ranks_here = lax.dynamic_slice_in_dim(ranks, lax.axis_index("x") * lay, lay)
    return finish(ranks_here, inv, later, got, last)


def solution(mesh):
    wide, lines = mesh.devices.shape
    groups = 8
    planes = wide // groups
    fine = Mesh(mesh.devices.reshape(planes, groups // CORES, CORES, lines), ROW + ("x",))
    in_specs = (
        P("x", ROW, None),
        P("x", ROW, None),
        P(None, ROW),
        P("x", ROW, None),
        P(),
    )
    return jax.shard_map(
        functools.partial(per_device, planes, groups, lines),
        mesh=fine,
        in_specs=in_specs,
        out_specs=P("x", None, ROW),
        check_vma=False,
    )
```

```python
import functools

import jax
import jax.numpy as jnp
from jax import lax
from jax.experimental import pallas as pl
from jax.experimental.pallas import tpu as pltpu
from jax.sharding import Mesh
from jax.sharding import PartitionSpec as P

ROW = ("z", "y", "c")
CORES = 2
STEP = 4
SMALL = pltpu.CompilerParams(vmem_limit_bytes=8 * 1024 * 1024)
LARGE = pltpu.CompilerParams(vmem_limit_bytes=24 * 1024 * 1024)
SCALARS = pl.BlockSpec(memory_space=pltpu.SMEM)
ANYWHERE = pl.BlockSpec(memory_space=pl.ANY)


def dot32(a, b, dims=((1,), (0,))):
    return lax.dot_general(
        a, b, (dims, ((), ())), precision=lax.Precision.HIGHEST, preferred_element_type=jnp.float32
    )


def cut_kernel(*refs):
    w_refs, o_ref = refs[1:-1], refs[-1]
    groups, cols = o_ref.shape[0], o_ref.shape[3] // len(w_refs)
    for i, w_ref in enumerate(w_refs):
        for g in range(groups):
            here = slice(g * cols, (g + 1) * cols)
            o_ref[g, :, :, i * cols : (i + 1) * cols] = w_ref[:, :, here]


def cut_by_owner(pos, weights, groups, planes):
    lay, rows, width = weights.shape
    cols = width // (groups * planes)
    ways = 2

    def place(i):
        return lambda z, pos: (0, 0, lax.rem(pos[0] + ways * z + i, planes))

    spec = pltpu.PrefetchScalarGridSpec(
        num_scalar_prefetch=1,
        grid=(planes // ways,),
        in_specs=[pl.BlockSpec((lay, rows, groups * cols), place(i)) for i in range(ways)],
        out_specs=pl.BlockSpec((groups, lay, rows, cols * ways), lambda z, pos: (0, 0, 0, z)),
    )
    return pl.pallas_call(
        cut_kernel,
        grid_spec=spec,
        out_shape=pltpu.HBM((groups, lay, rows, planes * cols), weights.dtype),
        compiler_params=LARGE,
        name="cut_by_owner",
    )(pos, *[weights] * ways)


def after_kernel(*refs):
    del refs


def after(first, arrays):
    return pl.pallas_call(
        after_kernel,
        in_specs=[ANYWHERE] * (len(arrays) + len(first)),
        out_specs=[ANYWHERE] * len(arrays),
        out_shape=[pltpu.HBM(a.shape, a.dtype) for a in arrays],
        input_output_aliases={i: i for i in range(len(arrays))},
        name="after",
    )(*arrays, *first)


def group_back(pos_ref, k, groups):
    lines = groups // CORES
    y = lax.rem(pos_ref[1] - k // CORES + lines, lines)
    c = lax.rem(pos_ref[2] + k % CORES, CORES)
    return y * CORES + c


def residual_kernel(count, _, *refs):
    w_refs, (c_ref, d_ref, b_ref, m_ref) = refs[:count], refs[count : count + 4]
    r_ref, keep_ref, send_ref, acc_ref, all_ref = refs[-5:]
    step, _, cols = b_ref.shape
    rows = w_refs[0].shape[2]
    layer, plane = pl.program_id(0), pl.program_id(1)

    @pl.when((layer == 0) & (plane == 0))
    def _():
        acc_ref[...] = jnp.zeros_like(acc_ref)

    @pl.when(plane == 0)
    def _():
        for k in range(count):
            all_ref[k * rows : (k + 1) * rows] = (c_ref, d_ref)[k % CORES][k // CORES, 0]

    total = None
    for i in range(step):
        here = slice(i * cols, (i + 1) * cols)
        low = jnp.dot(all_ref[...], b_ref[i], preferred_element_type=jnp.float32)
        w = jnp.concatenate([w_ref[0, 0, :, here] for w_ref in w_refs], axis=0)
        res = (w.astype(jnp.float32) - low).astype(jnp.bfloat16)
        r_ref[0, i] = res
        part = jnp.dot(res, m_ref[i, 0], preferred_element_type=jnp.float32)
        total = part if total is None else total + part
    acc_ref[...] += total

    @pl.when((layer == pl.num_programs(0) - 1) & (plane == pl.num_programs(1) - 1))
    def _():
        for k in range(count):
            (keep_ref, send_ref)[k % CORES][k // CORES] = acc_ref[k * rows : (k + 1) * rows]


def residual_and_sketch(pos, half, halves, w, near, others, maps, basis, before):
    groups, lay, rows, width = w.shape
    count = groups // halves
    planes, _, _, sw = maps.shape
    rank = near.shape[3]
    cols = width // planes
    tall = count * rows
    coeff = pl.BlockSpec((count // CORES, 1, rows, rank), lambda l, z, pos: (half, l, 0, 0))
    kept = [] if before is None else [before]

    def place(k):
        return lambda l, z, pos: (group_back(pos, half * count + k, groups), l, 0, z)

    spec = pltpu.PrefetchScalarGridSpec(
        num_scalar_prefetch=1,
        grid=(lay, planes // STEP),
        in_specs=[pl.BlockSpec((1, 1, rows, cols * STEP), place(k)) for k in range(count)]
        + [
            coeff,
            coeff,
            pl.BlockSpec((STEP, rank, cols), lambda l, z, pos: (z, 0, 0)),
            pl.BlockSpec((STEP, 1, cols, sw), lambda l, z, pos: (z, l, 0, 0)),
        ]
        + [ANYWHERE] * len(kept),
        out_specs=[pl.BlockSpec((1, STEP, tall, cols), lambda l, z, pos: (l, z, half, 0))]
        + [pl.BlockSpec((count // CORES, rows, sw), lambda l, z, pos: (0, 0, 0))] * CORES,
        scratch_shapes=[
            pltpu.VMEM((tall, sw), jnp.float32),
            pltpu.VMEM((tall, rank), jnp.bfloat16),
        ],
    )
    return pl.pallas_call(
        functools.partial(residual_kernel, count),
        grid_spec=spec,
        out_shape=[jax.ShapeDtypeStruct((lay, planes, halves * tall, cols), jnp.bfloat16)]
        + [jax.ShapeDtypeStruct((count // CORES, rows, sw), jnp.float32)] * CORES,
        input_output_aliases={count + 5: 0} if kept else {},
        compiler_params=LARGE,
        name="residual_and_sketch",
    )(pos, *[w] * count, near, others, basis, maps, *kept)


def gram_kernel(pos_ref, near_ref, other_ref, both_ref, g_ref, t_ref):
    ys = near_ref.shape[0]
    sketch = [ref[k] for k in range(ys) for ref in (near_ref, other_ref)]
    sketch = jnp.concatenate(sketch, axis=0)
    share, sw = g_ref.shape
    t_ref[...] = sketch.T
    at = pl.multiple_of((pos_ref[3] * CORES + pos_ref[2]) * share, share)
    g_ref[...] = dot32(t_ref[pl.ds(at, share)], sketch)
    high = t_ref[...].astype(jnp.bfloat16)
    both_ref[:sw] = high
    both_ref[sw:] = (t_ref[...] - high.astype(jnp.float32)).astype(jnp.bfloat16)


def stack_and_gram(pos, near, others, lines):
    ys, rows, sw = near.shape
    tall = rows * ys * CORES
    return pl.pallas_call(
        gram_kernel,
        in_specs=[SCALARS] + [pl.BlockSpec(near.shape, lambda: (0, 0, 0))] * CORES,
        out_shape=[
            jax.ShapeDtypeStruct((2 * sw, tall), jnp.bfloat16),
            jax.ShapeDtypeStruct((sw // (CORES * lines), sw), jnp.float32),
        ],
        scratch_shapes=[pltpu.VMEM((sw, tall), jnp.float32)],
        compiler_params=SMALL,
        name="stack_and_gram",
    )(pos, near, others)


def project_kernel(both_ref, *refs):
    r_refs, o_refs = refs[:4], refs[4:]
    sw = both_ref.shape[0] // 2
    for i, r_ref in enumerate(r_refs):
        out = jnp.dot(both_ref[...], r_ref[0, 0], preferred_element_type=jnp.float32)
        o_refs[i % 2][i // 2] = out[:sw] + out[sw:]


def project(both, residual, first, rounds):
    lay, planes, rows, cols = residual.shape
    sw = both.shape[0] // 2
    mid = planes // 2
    places = (
        lambda r: (0, mid - first - r, 0, 0),
        lambda r: (0, lax.rem(mid + 1 + first + r, planes), 0, 0),
        lambda r: (1, mid - 1 - first - r, 0, 0),
        lambda r: (1, mid + first + r, 0, 0),
    )
    return pl.pallas_call(
        project_kernel,
        grid=(rounds,),
        in_specs=[pl.BlockSpec(both.shape, lambda r: (0, 0))]
        + [pl.BlockSpec((1, 1, rows, cols), place) for place in places],
        out_specs=[pl.BlockSpec((lay, sw, cols), lambda r: (r, 0, 0))] * 2,
        out_shape=[jax.ShapeDtypeStruct((rounds * lay, sw, cols), jnp.float32)] * 2,
        compiler_params=LARGE,
        name="project",
    )(both, *[residual] * len(places))


def factor_block(a):
    n = a.shape[0]
    four = 4
    row = lax.broadcasted_iota(jnp.int32, (n, n), 0)
    col = lax.broadcasted_iota(jnp.int32, (n, n), 1)
    left, right = a, jnp.where(row == col, 1.0, 0.0)
    done = []
    for j in range(0, n, four):
        r = j % 8
        if j and r == 0:
            left, right = left[8:], right[8:]
        mults = [
            jnp.broadcast_to(left[:, j + k : j + k + 1], left.shape) for k in range(four)
        ]
        lines = []
        for k in range(four):
            here = slice(r + k, r + k + 1)
            lower, upper = left[here], right[here]
            mult = mults[k]
            for m, (done_left, done_right) in enumerate(lines):
                weight = mults[m][here]
                lower = lower - weight * done_left
                upper = upper - weight * done_right
                mult = mult - mults[m] * mults[m][here]
            pivot = lax.rsqrt(mult[here])
            mults[k] = mult * pivot
            lines.append((lower * pivot, upper * pivot))
        for k in range(four):
            left = left - mults[k] * lines[k][0]
            right = right - mults[k] * lines[k][1]
            done.append(lines[k][1])
    return jnp.concatenate(done, axis=0)


def upper_kernel(pos_ref, mine_ref, other_ref, *refs):
    inv_ref, cross_ref, rest_ref, g_ref = refs[-4:]
    lines, share, _ = mine_ref.shape
    half = inv_ref.shape[0]
    for k in range(lines):
        x = lax.rem(pos_ref[3] - k + lines, lines) * CORES
        for c, ref in ((pos_ref[2], mine_ref), (1 - pos_ref[2], other_ref)):
            g_ref[pl.ds(pl.multiple_of((x + c) * share, share), share)] = ref[k]
    inv = factor_block(g_ref[:half, :half])
    panel = dot32(g_ref[half:, :half], inv, ((1,), (1,)))
    inv_ref[...] = inv
    cross_ref[...] = dot32(panel, inv)
    rest_ref[...] = g_ref[half:, half:] - dot32(panel, panel, ((1,), (1,)))


def upper_factor(pos, mine, other, first):
    lines, share, sw = mine.shape
    half = sw // 2
    return pl.pallas_call(
        upper_kernel,
        in_specs=[SCALARS]
        + [pl.BlockSpec(mine.shape, lambda: (0, 0, 0))] * 2
        + [ANYWHERE] * len(first),
        out_shape=[jax.ShapeDtypeStruct((half, half), jnp.float32)] * 3,
        scratch_shapes=[pltpu.VMEM((sw, sw), jnp.float32)],
        compiler_params=SMALL,
        name="upper_factor",
    )(pos, mine, other, *first)


def lower_kernel(inv_ref, cross_ref, rest_ref, *refs):
    o_ref = refs[-1]
    half = inv_ref.shape[0]
    inv = factor_block(rest_ref[...])
    o_ref[:half, :half] = inv_ref[...]
    o_ref[:half, half:] = jnp.zeros_like(inv)
    o_ref[half:, :half] = -dot32(inv, cross_ref[...])
    o_ref[half:, half:] = inv


def lower_factor(inv, cross, rest, first):
    full = 2 * inv.shape[0]
    return pl.pallas_call(
        lower_kernel,
        in_specs=[pl.BlockSpec(inv.shape, lambda: (0, 0))] * 3 + [ANYWHERE] * len(first),
        out_shape=jax.ShapeDtypeStruct((full, full), jnp.float32),
        compiler_params=SMALL,
        name="lower_factor",
    )(inv, cross, rest, *first)


def sum_kernel(*refs):
    refs[-1][...] = refs[0][...] + refs[1][...]


def add_after(a, b, first):
    whole = pl.BlockSpec(a.shape, lambda: (0, 0))
    return pl.pallas_call(
        sum_kernel,
        in_specs=[whole] * 2 + [ANYWHERE] * len(first),
        out_specs=whole,
        out_shape=jax.ShapeDtypeStruct(a.shape, a.dtype),
        compiler_params=SMALL,
        name="add_after",
    )(a, b, *first)


def ordered_kernel(n, pos_ref, *refs):
    parts, (o_ref, all_ref) = refs[:n], refs[-2:]
    for k, ref in enumerate(parts):
        all_ref[lax.rem(pos_ref[0] - k + 2 * n, n)] = ref[...]
    total = all_ref[0]
    for k in range(1, n):
        total = total + all_ref[k]
    o_ref[...] = total


def ordered_sum(pos, parts, first):
    shape = parts[0].shape
    return pl.pallas_call(
        functools.partial(ordered_kernel, len(parts)),
        in_specs=[SCALARS]
        + [pl.BlockSpec(shape, lambda: (0, 0))] * len(parts)
        + [ANYWHERE] * len(first),
        out_shape=jax.ShapeDtypeStruct(shape, jnp.float32),
        scratch_shapes=[pltpu.VMEM((len(parts), *shape), jnp.float32)],
        compiler_params=SMALL,
        name="ordered_sum",
    )(pos, *parts, *first)


def add_kernel(*refs):
    refs[-2][...] = refs[0][...] + refs[2][...]
    refs[-1][...] = refs[1][...] + refs[3][...]


def ring_add(later, got, r, first):
    rounds, (lay, sw, cols) = later[0].shape[0] // got[0].shape[0], got[0].shape
    one = r == rounds - 1
    n = 1 if one else lay
    where = (0, 1) if one else (0, 0)
    return pl.pallas_call(
        add_kernel,
        grid=(1,),
        in_specs=[pl.BlockSpec((n, sw, cols), lambda i, w=w: (lay // n * r + w, 0, 0)) for w in where]
        + [pl.BlockSpec((n, sw, cols), lambda i, w=w: (w, 0, 0)) for w in where]
        + [ANYWHERE] * len(first),
        out_specs=[pl.BlockSpec((n, sw, cols), lambda i: (0, 0, 0))] * 2,
        out_shape=[jax.ShapeDtypeStruct((n, sw, cols), jnp.float32)] * 2,
        compiler_params=SMALL,
        name="ring_add",
    )(*later, *got, *first)


def apply_kernel(inv_ref, later_ref, got_ref, o_ref):
    o_ref[0] = dot32(inv_ref[...], later_ref[0] + got_ref[0])


def apply_factor(inv, later, got, l):
    lay, sw, cols = got.shape
    end = later.shape[0] - lay + l
    return pl.pallas_call(
        apply_kernel,
        grid=(1,),
        in_specs=[
            pl.BlockSpec((sw, sw), lambda i: (0, 0)),
            pl.BlockSpec((1, sw, cols), lambda i: (end, 0, 0)),
            pl.BlockSpec((1, sw, cols), lambda i: (l, 0, 0)),
        ],
        out_specs=pl.BlockSpec((1, sw, cols), lambda i: (0, 0, 0)),
        out_shape=jax.ShapeDtypeStruct((1, sw, cols), jnp.float32),
        compiler_params=SMALL,
        name="apply_factor",
    )(inv, later, got)


def finish_kernel(ranks_ref, *refs):
    o_ref = refs[-1]
    for l in range(o_ref.shape[0]):
        out = refs[2 * l][0] + refs[2 * l + 1][0]
        kept = lax.broadcasted_iota(jnp.int32, out.shape, 0) < ranks_ref[l]
        o_ref[l] = jnp.where(kept, out, 0.0)


def finish(ranks, pairs):
    _, sw, cols = pairs[0].shape
    return pl.pallas_call(
        finish_kernel,
        in_specs=[SCALARS] + [pl.BlockSpec((1, sw, cols), lambda: (0, 0, 0))] * len(pairs),
        out_shape=jax.ShapeDtypeStruct((len(pairs) // 2, sw, cols), jnp.float32),
        compiler_params=SMALL,
        name="finish",
    )(ranks, *pairs)


def shift(x, axis, size, k):
    return lax.ppermute(x, axis, [(i, (i + k) % size) for i in range(size)])


def added(parts):
    return sum(parts[1:], parts[0])


def ring_gather(arrays, axis, size):
    got = [{0: x} for x in arrays]
    up, down = list(arrays), list(arrays)
    for k in range(1, size // 2 + 1):
        for i in range(len(arrays)):
            got[i][k] = up[i] = shift(up[i], axis, size, -1)
            if k < size - k:
                got[i][size - k] = down[i] = shift(down[i], axis, size, 1)
    return [jnp.stack([g[k] for k in range(size)]) for g in got]


def per_device(planes, groups, lines, weights, coeffs, basis, sketch_map, ranks):
    lay = weights.shape[0]
    ys = groups // CORES
    pos = jnp.stack([lax.axis_index(a) for a in (*ROW, "x")]).astype(jnp.int32)
    near = jnp.stack([coeffs] + [shift(coeffs, "y", ys, k) for k in range(1, ys)])
    all_maps, all_basis = ring_gather((sketch_map, basis), "z", planes)
    weights = pltpu.with_memory_space_constraint(weights, pltpu.HBM)
    (cut,) = after([near], [cut_by_owner(pos, weights, groups, planes)])
    others = shift(near, "c", CORES, 1)
    w = lax.all_to_all(cut, ("y", "c"), 0, 0, tiled=True)
    halves, residual, parts = 1, None, []
    for half in range(halves):
        residual, keep, send = residual_and_sketch(
            pos, half, halves, w, near, others, all_maps, all_basis, residual
        )
        got = shift(send, "c", CORES, 1)
        parts += [keep[i] + got[i] for i in range(ys // halves)]
    mine = added([parts[0]] + [shift(parts[k], "y", ys, -k) for k in range(1, ys)])
    mine = added([mine] + [shift(mine, "x", lines, k) for k in range(1, lines)])
    rows_near = jnp.stack([mine] + [shift(mine, "y", ys, k) for k in range(1, ys)])
    both, gram = stack_and_gram(pos, rows_near, shift(rows_near, "c", CORES, 1), lines)

    across = shift(gram, "z", planes, planes // 2)
    start = project(both, residual, 0, 1)
    later = project(both, residual, 1, planes // 2 - 1)
    gram = add_after(gram, across, start)
    start = after([gram], start)
    gram = ordered_sum(pos, [gram] + [shift(gram, "z", planes, k) for k in (1, 2, -1)], [])
    summed = gram
    gram = jnp.stack([gram] + [shift(gram, "x", lines, k) for k in range(1, lines)])
    other = shift(gram, "c", CORES, 1)

    def send_both(pair):
        return shift(pair[0], "z", planes, 1), shift(pair[1], "z", planes, -1)

    sent = ring_add(later, send_both(start), 0, [summed])
    sent = ring_add(later, send_both(sent), 1, [other])
    up, down = send_both(sent)
    upper = upper_factor(pos, gram, other, sent)
    inv = lower_factor(*upper, [])
    last0 = shift(apply_factor(inv, later[0], up, 0), "z", planes, 1)
    last1 = shift(apply_factor(inv, later[1], down, 1), "z", planes, -1)
    rest0 = apply_factor(inv, later[1], down, 0)
    rest1 = apply_factor(inv, later[0], up, 1)
    ranks_here = lax.dynamic_slice_in_dim(ranks, lax.axis_index("x") * lay, lay)
    return finish(ranks_here, (last0, rest0, last1, rest1))


def solution(mesh):
    wide, lines = mesh.devices.shape
    groups = 8
    planes = wide // groups
    fine = Mesh(mesh.devices.reshape(planes, groups // CORES, CORES, lines), ROW + ("x",))
    in_specs = (
        P("x", ROW, None),
        P("x", ROW, None),
        P(None, ROW),
        P("x", ROW, None),
        P(),
    )
    return jax.shard_map(
        functools.partial(per_device, planes, groups, lines),
        mesh=fine,
        in_specs=in_specs,
        out_specs=P("x", None, ROW),
        check_vma=False,
    )
```

```python
import functools

import jax
import jax.numpy as jnp
from jax import lax
from jax.experimental import pallas as pl
from jax.experimental.pallas import tpu as pltpu
from jax.sharding import Mesh
from jax.sharding import PartitionSpec as P

ROW = ("z", "y", "c")
CORES = 2
STEP = 4
SMALL = pltpu.CompilerParams(vmem_limit_bytes=8 * 1024 * 1024)
LARGE = pltpu.CompilerParams(vmem_limit_bytes=24 * 1024 * 1024)
SCALARS = pl.BlockSpec(memory_space=pltpu.SMEM)
ANYWHERE = pl.BlockSpec(memory_space=pl.ANY)


def dot32(a, b, dims=((1,), (0,))):
    return lax.dot_general(
        a, b, (dims, ((), ())), precision=lax.Precision.HIGHEST, preferred_element_type=jnp.float32
    )


def cut_kernel(*refs):
    w_refs, o_ref = refs[1:-1], refs[-1]
    groups, cols = o_ref.shape[0], o_ref.shape[3] // len(w_refs)
    for i, w_ref in enumerate(w_refs):
        for g in range(groups):
            here = slice(g * cols, (g + 1) * cols)
            o_ref[g, :, :, i * cols : (i + 1) * cols] = w_ref[:, :, here]


def cut_by_owner(pos, weights, groups, planes):
    lay, rows, width = weights.shape
    cols = width // (groups * planes)
    ways = 4

    def place(i):
        return lambda z, pos: (0, 0, lax.rem(pos[0] + ways * z + i, planes))

    spec = pltpu.PrefetchScalarGridSpec(
        num_scalar_prefetch=1,
        grid=(planes // ways,),
        in_specs=[pl.BlockSpec((lay, rows, groups * cols), place(i)) for i in range(ways)],
        out_specs=pl.BlockSpec((groups, lay, rows, cols * ways), lambda z, pos: (0, 0, 0, z)),
    )
    return pl.pallas_call(
        cut_kernel,
        grid_spec=spec,
        out_shape=pltpu.HBM((groups, lay, rows, planes * cols), weights.dtype),
        compiler_params=LARGE,
        name="cut_by_owner",
    )(pos, *[weights] * ways)


def after_kernel(*refs):
    del refs


def after(first, arrays):
    return pl.pallas_call(
        after_kernel,
        in_specs=[ANYWHERE] * (len(arrays) + len(first)),
        out_specs=[ANYWHERE] * len(arrays),
        out_shape=[pltpu.HBM(a.shape, a.dtype) for a in arrays],
        input_output_aliases={i: i for i in range(len(arrays))},
        name="after",
    )(*arrays, *first)


def group_back(pos_ref, k, groups):
    lines = groups // CORES
    y = lax.rem(pos_ref[1] - k // CORES + lines, lines)
    c = lax.rem(pos_ref[2] + k % CORES, CORES)
    return y * CORES + c


def residual_kernel(count, _, *refs):
    w_refs, (c_ref, d_ref, b_ref, m_ref) = refs[:count], refs[count : count + 4]
    r_ref, keep_ref, send_ref, acc_ref, all_ref = refs[-5:]
    step, _, cols = b_ref.shape
    rows = w_refs[0].shape[2]
    layer, plane = pl.program_id(0), pl.program_id(1)

    @pl.when((layer == 0) & (plane == 0))
    def _():
        acc_ref[...] = jnp.zeros_like(acc_ref)

    @pl.when(plane == 0)
    def _():
        for k in range(count):
            all_ref[k * rows : (k + 1) * rows] = (c_ref, d_ref)[k % CORES][k // CORES, 0]

    total = None
    for i in range(step):
        here = slice(i * cols, (i + 1) * cols)
        low = jnp.dot(all_ref[...], b_ref[i], preferred_element_type=jnp.float32)
        w = jnp.concatenate([w_ref[0, 0, :, here] for w_ref in w_refs], axis=0)
        res = (w.astype(jnp.float32) - low).astype(jnp.bfloat16)
        r_ref[0, i] = res
        part = jnp.dot(res, m_ref[i, 0], preferred_element_type=jnp.float32)
        total = part if total is None else total + part
    acc_ref[...] += total

    @pl.when((layer == pl.num_programs(0) - 1) & (plane == pl.num_programs(1) - 1))
    def _():
        for k in range(count):
            (keep_ref, send_ref)[k % CORES][k // CORES] = acc_ref[k * rows : (k + 1) * rows]


def residual_and_sketch(pos, half, halves, w, near, others, maps, basis, before):
    groups, lay, rows, width = w.shape
    count = groups // halves
    planes, _, _, sw = maps.shape
    rank = near.shape[3]
    cols = width // planes
    tall = count * rows
    coeff = pl.BlockSpec((count // CORES, 1, rows, rank), lambda l, z, pos: (half, l, 0, 0))
    kept = [] if before is None else [before]

    def place(k):
        return lambda l, z, pos: (group_back(pos, half * count + k, groups), l, 0, z)

    spec = pltpu.PrefetchScalarGridSpec(
        num_scalar_prefetch=1,
        grid=(lay, planes // STEP),
        in_specs=[pl.BlockSpec((1, 1, rows, cols * STEP), place(k)) for k in range(count)]
        + [
            coeff,
            coeff,
            pl.BlockSpec((STEP, rank, cols), lambda l, z, pos: (z, 0, 0)),
            pl.BlockSpec((STEP, 1, cols, sw), lambda l, z, pos: (z, l, 0, 0)),
        ]
        + [ANYWHERE] * len(kept),
        out_specs=[pl.BlockSpec((1, STEP, tall, cols), lambda l, z, pos: (l, z, half, 0))]
        + [pl.BlockSpec((count // CORES, rows, sw), lambda l, z, pos: (0, 0, 0))] * CORES,
        scratch_shapes=[
            pltpu.VMEM((tall, sw), jnp.float32),
            pltpu.VMEM((tall, rank), jnp.bfloat16),
        ],
    )
    return pl.pallas_call(
        functools.partial(residual_kernel, count),
        grid_spec=spec,
        out_shape=[jax.ShapeDtypeStruct((lay, planes, halves * tall, cols), jnp.bfloat16)]
        + [jax.ShapeDtypeStruct((count // CORES, rows, sw), jnp.float32)] * CORES,
        input_output_aliases={count + 5: 0} if kept else {},
        compiler_params=LARGE,
        name="residual_and_sketch",
    )(pos, *[w] * count, near, others, basis, maps, *kept)


def gram_kernel(pos_ref, near_ref, other_ref, both_ref, g_ref, t_ref):
    ys = near_ref.shape[0]
    sketch = [ref[k] for k in range(ys) for ref in (near_ref, other_ref)]
    sketch = jnp.concatenate(sketch, axis=0)
    share, sw = g_ref.shape
    t_ref[...] = sketch.T
    at = pl.multiple_of((pos_ref[3] * CORES + pos_ref[2]) * share, share)
    g_ref[...] = dot32(t_ref[pl.ds(at, share)], sketch)
    high = t_ref[...].astype(jnp.bfloat16)
    both_ref[:sw] = high
    both_ref[sw:] = (t_ref[...] - high.astype(jnp.float32)).astype(jnp.bfloat16)


def stack_and_gram(pos, near, others, lines):
    ys, rows, sw = near.shape
    tall = rows * ys * CORES
    return pl.pallas_call(
        gram_kernel,
        in_specs=[SCALARS] + [pl.BlockSpec(near.shape, lambda: (0, 0, 0))] * CORES,
        out_shape=[
            jax.ShapeDtypeStruct((2 * sw, tall), jnp.bfloat16),
            jax.ShapeDtypeStruct((sw // (CORES * lines), sw), jnp.float32),
        ],
        scratch_shapes=[pltpu.VMEM((sw, tall), jnp.float32)],
        compiler_params=SMALL,
        name="stack_and_gram",
    )(pos, near, others)


def project_kernel(both_ref, *refs):
    r_refs, o_refs = refs[:4], refs[4:]
    sw = both_ref.shape[0] // 2
    for i, r_ref in enumerate(r_refs):
        out = jnp.dot(both_ref[...], r_ref[0, 0], preferred_element_type=jnp.float32)
        o_refs[i % 2][i // 2] = out[:sw] + out[sw:]


def project(both, residual, first, rounds):
    lay, planes, rows, cols = residual.shape
    sw = both.shape[0] // 2
    mid = planes // 2
    places = (
        lambda r: (0, mid - first - r, 0, 0),
        lambda r: (0, lax.rem(mid + 1 + first + r, planes), 0, 0),
        lambda r: (1, mid - 1 - first - r, 0, 0),
        lambda r: (1, mid + first + r, 0, 0),
    )
    return pl.pallas_call(
        project_kernel,
        grid=(rounds,),
        in_specs=[pl.BlockSpec(both.shape, lambda r: (0, 0))]
        + [pl.BlockSpec((1, 1, rows, cols), place) for place in places],
        out_specs=[pl.BlockSpec((lay, sw, cols), lambda r: (r, 0, 0))] * 2,
        out_shape=[jax.ShapeDtypeStruct((rounds * lay, sw, cols), jnp.float32)] * 2,
        compiler_params=LARGE,
        name="project",
    )(both, *[residual] * len(places))


def factor_block(a):
    n = a.shape[0]
    four = 4
    row = lax.broadcasted_iota(jnp.int32, (n, n), 0)
    col = lax.broadcasted_iota(jnp.int32, (n, n), 1)
    left, right = a, jnp.where(row == col, 1.0, 0.0)
    done = []
    for j in range(0, n, four):
        r = j % 8
        if j and r == 0:
            left, right = left[8:], right[8:]
        mults = [
            jnp.broadcast_to(left[:, j + k : j + k + 1], left.shape) for k in range(four)
        ]
        lines = []
        for k in range(four):
            here = slice(r + k, r + k + 1)
            lower, upper = left[here], right[here]
            mult = mults[k]
            for m, (done_left, done_right) in enumerate(lines):
                weight = mults[m][here]
                lower = lower - weight * done_left
                upper = upper - weight * done_right
                mult = mult - mults[m] * mults[m][here]
            pivot = lax.rsqrt(mult[here])
            mults[k] = mult * pivot
            lines.append((lower * pivot, upper * pivot))
        for k in range(four):
            left = left - mults[k] * lines[k][0]
            right = right - mults[k] * lines[k][1]
            done.append(lines[k][1])
    return jnp.concatenate(done, axis=0)


def upper_kernel(pos_ref, mine_ref, other_ref, *refs):
    inv_ref, cross_ref, rest_ref, g_ref = refs[-4:]
    lines, share, _ = mine_ref.shape
    half = inv_ref.shape[0]
    for k in range(lines):
        x = lax.rem(pos_ref[3] - k + lines, lines) * CORES
        for c, ref in ((pos_ref[2], mine_ref), (1 - pos_ref[2], other_ref)):
            g_ref[pl.ds(pl.multiple_of((x + c) * share, share), share)] = ref[k]
    inv = factor_block(g_ref[:half, :half])
    panel = dot32(g_ref[half:, :half], inv, ((1,), (1,)))
    inv_ref[...] = inv
    cross_ref[...] = dot32(panel, inv)
    rest_ref[...] = g_ref[half:, half:] - dot32(panel, panel, ((1,), (1,)))


def upper_factor(pos, mine, other, first):
    lines, share, sw = mine.shape
    half = sw // 2
    return pl.pallas_call(
        upper_kernel,
        in_specs=[SCALARS]
        + [pl.BlockSpec(mine.shape, lambda: (0, 0, 0))] * 2
        + [ANYWHERE] * len(first),
        out_shape=[jax.ShapeDtypeStruct((half, half), jnp.float32)] * 3,
        scratch_shapes=[pltpu.VMEM((sw, sw), jnp.float32)],
        compiler_params=SMALL,
        name="upper_factor",
    )(pos, mine, other, *first)


def lower_kernel(inv_ref, cross_ref, rest_ref, *refs):
    o_ref = refs[-1]
    half = inv_ref.shape[0]
    inv = factor_block(rest_ref[...])
    o_ref[:half, :half] = inv_ref[...]
    o_ref[:half, half:] = jnp.zeros_like(inv)
    o_ref[half:, :half] = -dot32(inv, cross_ref[...])
    o_ref[half:, half:] = inv


def lower_factor(inv, cross, rest, first):
    full = 2 * inv.shape[0]
    return pl.pallas_call(
        lower_kernel,
        in_specs=[pl.BlockSpec(inv.shape, lambda: (0, 0))] * 3 + [ANYWHERE] * len(first),
        out_shape=jax.ShapeDtypeStruct((full, full), jnp.float32),
        compiler_params=SMALL,
        name="lower_factor",
    )(inv, cross, rest, *first)


def sum_kernel(*refs):
    refs[-1][...] = refs[0][...] + refs[1][...]


def add_after(a, b, first):
    whole = pl.BlockSpec(a.shape, lambda: (0, 0))
    return pl.pallas_call(
        sum_kernel,
        in_specs=[whole] * 2 + [ANYWHERE] * len(first),
        out_specs=whole,
        out_shape=jax.ShapeDtypeStruct(a.shape, a.dtype),
        compiler_params=SMALL,
        name="add_after",
    )(a, b, *first)


def ordered_kernel(n, pos_ref, *refs):
    parts, (o_ref, all_ref) = refs[:n], refs[-2:]
    for k, ref in enumerate(parts):
        all_ref[lax.rem(pos_ref[0] - k + 2 * n, n)] = ref[...]
    total = all_ref[0]
    for k in range(1, n):
        total = total + all_ref[k]
    o_ref[...] = total


def ordered_sum(pos, parts, first):
    shape = parts[0].shape
    return pl.pallas_call(
        functools.partial(ordered_kernel, len(parts)),
        in_specs=[SCALARS]
        + [pl.BlockSpec(shape, lambda: (0, 0))] * len(parts)
        + [ANYWHERE] * len(first),
        out_shape=jax.ShapeDtypeStruct(shape, jnp.float32),
        scratch_shapes=[pltpu.VMEM((len(parts), *shape), jnp.float32)],
        compiler_params=SMALL,
        name="ordered_sum",
    )(pos, *parts, *first)


def add_kernel(*refs):
    refs[-2][...] = refs[0][...] + refs[2][...]
    refs[-1][...] = refs[1][...] + refs[3][...]


def ring_add(later, got, r, first):
    rounds, (lay, sw, cols) = later[0].shape[0] // got[0].shape[0], got[0].shape
    one = r == rounds - 1
    n = 1 if one else lay
    where = (0, 1) if one else (0, 0)
    return pl.pallas_call(
        add_kernel,
        grid=(1,),
        in_specs=[pl.BlockSpec((n, sw, cols), lambda i, w=w: (lay // n * r + w, 0, 0)) for w in where]
        + [pl.BlockSpec((n, sw, cols), lambda i, w=w: (w, 0, 0)) for w in where]
        + [ANYWHERE] * len(first),
        out_specs=[pl.BlockSpec((n, sw, cols), lambda i: (0, 0, 0))] * 2,
        out_shape=[jax.ShapeDtypeStruct((n, sw, cols), jnp.float32)] * 2,
        compiler_params=SMALL,
        name="ring_add",
    )(*later, *got, *first)


def apply_kernel(inv_ref, later_ref, got_ref, o_ref):
    o_ref[0] = dot32(inv_ref[...], later_ref[0] + got_ref[0])


def apply_factor(inv, later, got, l):
    lay, sw, cols = got.shape
    end = later.shape[0] - lay + l
    return pl.pallas_call(
        apply_kernel,
        grid=(1,),
        in_specs=[
            pl.BlockSpec((sw, sw), lambda i: (0, 0)),
            pl.BlockSpec((1, sw, cols), lambda i: (end, 0, 0)),
            pl.BlockSpec((1, sw, cols), lambda i: (l, 0, 0)),
        ],
        out_specs=pl.BlockSpec((1, sw, cols), lambda i: (0, 0, 0)),
        out_shape=jax.ShapeDtypeStruct((1, sw, cols), jnp.float32),
        compiler_params=SMALL,
        name="apply_factor",
    )(inv, later, got)


def finish_kernel(ranks_ref, *refs):
    o_ref = refs[-1]
    for l in range(o_ref.shape[0]):
        out = refs[2 * l][0] + refs[2 * l + 1][0]
        kept = lax.broadcasted_iota(jnp.int32, out.shape, 0) < ranks_ref[l]
        o_ref[l] = jnp.where(kept, out, 0.0)


def finish(ranks, pairs):
    _, sw, cols = pairs[0].shape
    return pl.pallas_call(
        finish_kernel,
        in_specs=[SCALARS] + [pl.BlockSpec((1, sw, cols), lambda: (0, 0, 0))] * len(pairs),
        out_shape=jax.ShapeDtypeStruct((len(pairs) // 2, sw, cols), jnp.float32),
        compiler_params=SMALL,
        name="finish",
    )(ranks, *pairs)


def shift(x, axis, size, k):
    return lax.ppermute(x, axis, [(i, (i + k) % size) for i in range(size)])


def added(parts):
    return sum(parts[1:], parts[0])


def ring_gather(arrays, axis, size):
    got = [{0: x} for x in arrays]
    up, down = list(arrays), list(arrays)
    for k in range(1, size // 2 + 1):
        for i in range(len(arrays)):
            got[i][k] = up[i] = shift(up[i], axis, size, -1)
            if k < size - k:
                got[i][size - k] = down[i] = shift(down[i], axis, size, 1)
    return [jnp.stack([g[k] for k in range(size)]) for g in got]


def per_device(planes, groups, lines, weights, coeffs, basis, sketch_map, ranks):
    lay = weights.shape[0]
    ys = groups // CORES
    pos = jnp.stack([lax.axis_index(a) for a in (*ROW, "x")]).astype(jnp.int32)
    near = jnp.stack([coeffs] + [shift(coeffs, "y", ys, k) for k in range(1, ys)])
    gathered = ring_gather((sketch_map, basis), "z", planes)
    all_maps, all_basis = [pltpu.with_memory_space_constraint(x, pltpu.HBM) for x in gathered]
    weights = pltpu.with_memory_space_constraint(weights, pltpu.HBM)
    (cut,) = after([near], [cut_by_owner(pos, weights, groups, planes)])
    others = shift(near, "c", CORES, 1)
    w = lax.all_to_all(cut, ("y", "c"), 0, 0, tiled=True)
    halves, residual, parts = 1, None, []
    for half in range(halves):
        residual, keep, send = residual_and_sketch(
            pos, half, halves, w, near, others, all_maps, all_basis, residual
        )
        got = shift(send, "c", CORES, 1)
        parts += [keep[i] + got[i] for i in range(ys // halves)]
    mine = added([parts[0]] + [shift(parts[k], "y", ys, -k) for k in range(1, ys)])
    mine = added([mine] + [shift(mine, "x", lines, k) for k in range(1, lines)])
    rows_near = jnp.stack([mine] + [shift(mine, "y", ys, k) for k in range(1, ys)])
    both, gram = stack_and_gram(pos, rows_near, shift(rows_near, "c", CORES, 1), lines)

    across = shift(gram, "z", planes, planes // 2)
    start = project(both, residual, 0, 1)
    later = project(both, residual, 1, planes // 2 - 1)
    gram = add_after(gram, across, start)
    start = after([gram], start)
    gram = ordered_sum(pos, [gram] + [shift(gram, "z", planes, k) for k in (1, 2, -1)], [])
    summed = gram
    gram = jnp.stack([gram] + [shift(gram, "x", lines, k) for k in range(1, lines)])
    other = shift(gram, "c", CORES, 1)

    def send_both(pair):
        return shift(pair[0], "z", planes, 1), shift(pair[1], "z", planes, -1)

    sent = ring_add(later, send_both(start), 0, [summed])
    sent = ring_add(later, send_both(sent), 1, [other])
    up, down = send_both(sent)
    upper = upper_factor(pos, gram, other, sent)
    inv = lower_factor(*upper, [])
    last0 = shift(apply_factor(inv, later[0], up, 0), "z", planes, 1)
    last1 = shift(apply_factor(inv, later[1], down, 1), "z", planes, -1)
    rest0 = apply_factor(inv, later[1], down, 0)
    rest1 = apply_factor(inv, later[0], up, 1)
    ranks_here = lax.dynamic_slice_in_dim(ranks, lax.axis_index("x") * lay, lay)
    return finish(ranks_here, (last0, rest0, last1, rest1))


def solution(mesh):
    wide, lines = mesh.devices.shape
    groups = 8
    planes = wide // groups
    fine = Mesh(mesh.devices.reshape(planes, groups // CORES, CORES, lines), ROW + ("x",))
    in_specs = (
        P("x", ROW, None),
        P("x", ROW, None),
        P(None, ROW),
        P("x", ROW, None),
        P(),
    )
    return jax.shard_map(
        functools.partial(per_device, planes, groups, lines),
        mesh=fine,
        in_specs=in_specs,
        out_specs=P("x", None, ROW),
        check_vma=False,
    )
```

```python
import functools

import jax
import jax.numpy as jnp
from jax import lax
from jax.experimental import pallas as pl
from jax.experimental.pallas import tpu as pltpu
from jax.sharding import Mesh
from jax.sharding import PartitionSpec as P

ROW = ("z", "y", "c")
CORES = 2
STEP = 4
SMALL = pltpu.CompilerParams(vmem_limit_bytes=8 * 1024 * 1024)
LARGE = pltpu.CompilerParams(vmem_limit_bytes=24 * 1024 * 1024)
SCALARS = pl.BlockSpec(memory_space=pltpu.SMEM)
ANYWHERE = pl.BlockSpec(memory_space=pl.ANY)


def dot32(a, b, dims=((1,), (0,))):
    return lax.dot_general(
        a, b, (dims, ((), ())), precision=lax.Precision.HIGHEST, preferred_element_type=jnp.float32
    )


def cut_kernel(*refs):
    w_refs, o_ref = refs[1:-1], refs[-1]
    groups, cols = o_ref.shape[0], o_ref.shape[3] // len(w_refs)
    for i, w_ref in enumerate(w_refs):
        for g in range(groups):
            here = slice(g * cols, (g + 1) * cols)
            o_ref[g, :, :, i * cols : (i + 1) * cols] = w_ref[:, :, here]


def cut_by_owner(pos, weights, groups, planes):
    lay, rows, width = weights.shape
    cols = width // (groups * planes)
    ways = 4

    def place(i):
        return lambda z, pos: (0, 0, lax.rem(pos[0] + ways * z + i, planes))

    spec = pltpu.PrefetchScalarGridSpec(
        num_scalar_prefetch=1,
        grid=(planes // ways,),
        in_specs=[pl.BlockSpec((lay, rows, groups * cols), place(i)) for i in range(ways)],
        out_specs=pl.BlockSpec((groups, lay, rows, cols * ways), lambda z, pos: (0, 0, 0, z)),
    )
    return pl.pallas_call(
        cut_kernel,
        grid_spec=spec,
        out_shape=pltpu.HBM((groups, lay, rows, planes * cols), weights.dtype),
        compiler_params=LARGE,
        name="cut_by_owner",
    )(pos, *[weights] * ways)


def after_kernel(*refs):
    del refs


def after(first, arrays):
    return pl.pallas_call(
        after_kernel,
        in_specs=[ANYWHERE] * (len(arrays) + len(first)),
        out_specs=[ANYWHERE] * len(arrays),
        out_shape=[pltpu.HBM(a.shape, a.dtype) for a in arrays],
        input_output_aliases={i: i for i in range(len(arrays))},
        name="after",
    )(*arrays, *first)


def group_back(pos_ref, k, groups):
    lines = groups // CORES
    y = lax.rem(pos_ref[1] - k // CORES + lines, lines)
    c = lax.rem(pos_ref[2] + k % CORES, CORES)
    return y * CORES + c


def residual_kernel(count, _, *refs):
    w_refs, (c_ref, d_ref, b_ref, m_ref) = refs[:count], refs[count : count + 4]
    r_ref, keep_ref, send_ref, acc_ref, all_ref = refs[-5:]
    step, _, cols = b_ref.shape
    rows = w_refs[0].shape[2]
    layer, plane = pl.program_id(0), pl.program_id(1)

    @pl.when((layer == 0) & (plane == 0))
    def _():
        acc_ref[...] = jnp.zeros_like(acc_ref)

    @pl.when(plane == 0)
    def _():
        for k in range(count):
            all_ref[k * rows : (k + 1) * rows] = (c_ref, d_ref)[k % CORES][k // CORES, 0]

    total = None
    for i in range(step):
        here = slice(i * cols, (i + 1) * cols)
        low = jnp.dot(all_ref[...], b_ref[i], preferred_element_type=jnp.float32)
        w = jnp.concatenate([w_ref[0, 0, :, here] for w_ref in w_refs], axis=0)
        res = (w.astype(jnp.float32) - low).astype(jnp.bfloat16)
        r_ref[0, i] = res
        part = jnp.dot(res, m_ref[i, 0], preferred_element_type=jnp.float32)
        total = part if total is None else total + part
    acc_ref[...] += total

    @pl.when((layer == pl.num_programs(0) - 1) & (plane == pl.num_programs(1) - 1))
    def _():
        for k in range(count):
            (keep_ref, send_ref)[k % CORES][k // CORES] = acc_ref[k * rows : (k + 1) * rows]


def residual_and_sketch(pos, half, halves, w, near, others, maps, basis, before):
    groups, lay, rows, width = w.shape
    count = groups // halves
    planes, _, _, sw = maps.shape
    rank = near.shape[3]
    cols = width // planes
    tall = count * rows
    coeff = pl.BlockSpec((count // CORES, 1, rows, rank), lambda l, z, pos: (half, l, 0, 0))
    kept = [] if before is None else [before]

    def place(k):
        return lambda l, z, pos: (group_back(pos, half * count + k, groups), l, 0, z)

    spec = pltpu.PrefetchScalarGridSpec(
        num_scalar_prefetch=1,
        grid=(lay, planes // STEP),
        in_specs=[pl.BlockSpec((1, 1, rows, cols * STEP), place(k)) for k in range(count)]
        + [
            coeff,
            coeff,
            pl.BlockSpec((STEP, rank, cols), lambda l, z, pos: (z, 0, 0)),
            pl.BlockSpec((STEP, 1, cols, sw), lambda l, z, pos: (z, l, 0, 0)),
        ]
        + [ANYWHERE] * len(kept),
        out_specs=[pl.BlockSpec((1, STEP, tall, cols), lambda l, z, pos: (l, z, half, 0))]
        + [pl.BlockSpec((count // CORES, rows, sw), lambda l, z, pos: (0, 0, 0))] * CORES,
        scratch_shapes=[
            pltpu.VMEM((tall, sw), jnp.float32),
            pltpu.VMEM((tall, rank), jnp.bfloat16),
        ],
    )
    return pl.pallas_call(
        functools.partial(residual_kernel, count),
        grid_spec=spec,
        out_shape=[jax.ShapeDtypeStruct((lay, planes, halves * tall, cols), jnp.bfloat16)]
        + [jax.ShapeDtypeStruct((count // CORES, rows, sw), jnp.float32)] * CORES,
        input_output_aliases={count + 5: 0} if kept else {},
        compiler_params=LARGE,
        name="residual_and_sketch",
    )(pos, *[w] * count, near, others, basis, maps, *kept)


def gram_kernel(pos_ref, near_ref, other_ref, both_ref, g_ref, t_ref):
    ys = near_ref.shape[0]
    sketch = [ref[k] for k in range(ys) for ref in (near_ref, other_ref)]
    sketch = jnp.concatenate(sketch, axis=0)
    share, sw = g_ref.shape
    t_ref[...] = sketch.T
    at = pl.multiple_of((pos_ref[3] * CORES + pos_ref[2]) * share, share)
    g_ref[...] = dot32(t_ref[pl.ds(at, share)], sketch)
    high = t_ref[...].astype(jnp.bfloat16)
    both_ref[:sw] = high
    both_ref[sw:] = (t_ref[...] - high.astype(jnp.float32)).astype(jnp.bfloat16)


def stack_and_gram(pos, near, others, lines):
    ys, rows, sw = near.shape
    tall = rows * ys * CORES
    return pl.pallas_call(
        gram_kernel,
        in_specs=[SCALARS] + [pl.BlockSpec(near.shape, lambda: (0, 0, 0))] * CORES,
        out_shape=[
            jax.ShapeDtypeStruct((2 * sw, tall), jnp.bfloat16),
            jax.ShapeDtypeStruct((sw // (CORES * lines), sw), jnp.float32),
        ],
        scratch_shapes=[pltpu.VMEM((sw, tall), jnp.float32)],
        compiler_params=SMALL,
        name="stack_and_gram",
    )(pos, near, others)


def project_kernel(both_ref, *refs):
    r_refs, o_refs = refs[:4], refs[4:]
    sw = both_ref.shape[0] // 2
    for i, r_ref in enumerate(r_refs):
        out = jnp.dot(both_ref[...], r_ref[0, 0], preferred_element_type=jnp.float32)
        o_refs[i % 2][i // 2] = out[:sw] + out[sw:]


def project(both, residual, first, rounds):
    lay, planes, rows, cols = residual.shape
    sw = both.shape[0] // 2
    mid = planes // 2
    places = (
        lambda r: (0, mid - first - r, 0, 0),
        lambda r: (0, lax.rem(mid + 1 + first + r, planes), 0, 0),
        lambda r: (1, mid - 1 - first - r, 0, 0),
        lambda r: (1, mid + first + r, 0, 0),
    )
    return pl.pallas_call(
        project_kernel,
        grid=(rounds,),
        in_specs=[pl.BlockSpec(both.shape, lambda r: (0, 0))]
        + [pl.BlockSpec((1, 1, rows, cols), place) for place in places],
        out_specs=[pl.BlockSpec((lay, sw, cols), lambda r: (r, 0, 0))] * 2,
        out_shape=[jax.ShapeDtypeStruct((rounds * lay, sw, cols), jnp.float32)] * 2,
        compiler_params=LARGE,
        name="project",
    )(both, *[residual] * len(places))


def factor_block(a):
    n = a.shape[0]
    four = 4
    row = lax.broadcasted_iota(jnp.int32, (n, n), 0)
    col = lax.broadcasted_iota(jnp.int32, (n, n), 1)
    left, right = a, jnp.where(row == col, 1.0, 0.0)
    done = []
    for j in range(0, n, four):
        r = j % 8
        if j and r == 0:
            left, right = left[8:], right[8:]
        mults = [
            jnp.broadcast_to(left[:, j + k : j + k + 1], left.shape) for k in range(four)
        ]
        lines = []
        for k in range(four):
            here = slice(r + k, r + k + 1)
            lower, upper = left[here], right[here]
            mult = mults[k]
            for m, (done_left, done_right) in enumerate(lines):
                weight = mults[m][here]
                lower = lower - weight * done_left
                upper = upper - weight * done_right
                mult = mult - mults[m] * mults[m][here]
            pivot = lax.rsqrt(mult[here])
            mults[k] = mult * pivot
            lines.append((lower * pivot, upper * pivot))
        for k in range(four):
            left = left - mults[k] * lines[k][0]
            right = right - mults[k] * lines[k][1]
            done.append(lines[k][1])
    return jnp.concatenate(done, axis=0)


def upper_kernel(pos_ref, mine_ref, other_ref, *refs):
    inv_ref, cross_ref, rest_ref, g_ref = refs[-4:]
    lines, share, _ = mine_ref.shape
    half = inv_ref.shape[0]
    for k in range(lines):
        x = lax.rem(pos_ref[3] - k + lines, lines) * CORES
        for c, ref in ((pos_ref[2], mine_ref), (1 - pos_ref[2], other_ref)):
            g_ref[pl.ds(pl.multiple_of((x + c) * share, share), share)] = ref[k]
    inv = factor_block(g_ref[:half, :half])
    panel = dot32(g_ref[half:, :half], inv, ((1,), (1,)))
    inv_ref[...] = inv
    cross_ref[...] = dot32(panel, inv)
    rest_ref[...] = g_ref[half:, half:] - dot32(panel, panel, ((1,), (1,)))


def upper_factor(pos, mine, other, first):
    lines, share, sw = mine.shape
    half = sw // 2
    return pl.pallas_call(
        upper_kernel,
        in_specs=[SCALARS]
        + [pl.BlockSpec(mine.shape, lambda: (0, 0, 0))] * 2
        + [ANYWHERE] * len(first),
        out_shape=[jax.ShapeDtypeStruct((half, half), jnp.float32)] * 3,
        scratch_shapes=[pltpu.VMEM((sw, sw), jnp.float32)],
        compiler_params=SMALL,
        name="upper_factor",
    )(pos, mine, other, *first)


def lower_kernel(inv_ref, cross_ref, rest_ref, *refs):
    o_ref = refs[-1]
    half = inv_ref.shape[0]
    inv = factor_block(rest_ref[...])
    o_ref[:half, :half] = inv_ref[...]
    o_ref[:half, half:] = jnp.zeros_like(inv)
    o_ref[half:, :half] = -dot32(inv, cross_ref[...])
    o_ref[half:, half:] = inv


def lower_factor(inv, cross, rest, first):
    full = 2 * inv.shape[0]
    return pl.pallas_call(
        lower_kernel,
        in_specs=[pl.BlockSpec(inv.shape, lambda: (0, 0))] * 3 + [ANYWHERE] * len(first),
        out_shape=jax.ShapeDtypeStruct((full, full), jnp.float32),
        compiler_params=SMALL,
        name="lower_factor",
    )(inv, cross, rest, *first)


def sum_kernel(*refs):
    refs[-1][...] = refs[0][...] + refs[1][...]


def add_after(a, b, first):
    whole = pl.BlockSpec(a.shape, lambda: (0, 0))
    return pl.pallas_call(
        sum_kernel,
        in_specs=[whole] * 2 + [ANYWHERE] * len(first),
        out_specs=whole,
        out_shape=jax.ShapeDtypeStruct(a.shape, a.dtype),
        compiler_params=SMALL,
        name="add_after",
    )(a, b, *first)


def ordered_kernel(n, pos_ref, *refs):
    parts, (o_ref, all_ref) = refs[:n], refs[-2:]
    for k, ref in enumerate(parts):
        all_ref[lax.rem(pos_ref[0] - k + 2 * n, n)] = ref[...]
    total = all_ref[0]
    for k in range(1, n):
        total = total + all_ref[k]
    o_ref[...] = total


def ordered_sum(pos, parts, first):
    shape = parts[0].shape
    return pl.pallas_call(
        functools.partial(ordered_kernel, len(parts)),
        in_specs=[SCALARS]
        + [pl.BlockSpec(shape, lambda: (0, 0))] * len(parts)
        + [ANYWHERE] * len(first),
        out_shape=jax.ShapeDtypeStruct(shape, jnp.float32),
        scratch_shapes=[pltpu.VMEM((len(parts), *shape), jnp.float32)],
        compiler_params=SMALL,
        name="ordered_sum",
    )(pos, *parts, *first)


def add_kernel(*refs):
    refs[-2][...] = refs[0][...] + refs[2][...]
    refs[-1][...] = refs[1][...] + refs[3][...]


def ring_add(later, got, r, first):
    rounds, (lay, sw, cols) = later[0].shape[0] // got[0].shape[0], got[0].shape
    one = r == rounds - 1
    n = 1 if one else lay
    where = (0, 1) if one else (0, 0)
    return pl.pallas_call(
        add_kernel,
        grid=(1,),
        in_specs=[pl.BlockSpec((n, sw, cols), lambda i, w=w: (lay // n * r + w, 0, 0)) for w in where]
        + [pl.BlockSpec((n, sw, cols), lambda i, w=w: (w, 0, 0)) for w in where]
        + [ANYWHERE] * len(first),
        out_specs=[pl.BlockSpec((n, sw, cols), lambda i: (0, 0, 0))] * 2,
        out_shape=[jax.ShapeDtypeStruct((n, sw, cols), jnp.float32)] * 2,
        compiler_params=SMALL,
        name="ring_add",
    )(*later, *got, *first)


def apply_kernel(inv_ref, *refs):
    for i in range(2):
        refs[4 + i][0] = dot32(inv_ref[...], refs[2 * i][0] + refs[2 * i + 1][0])


def apply_factor(inv, pairs):
    specs, flat = [], []
    for l, (later, got) in enumerate(pairs):
        lay, sw, cols = got.shape
        end = later.shape[0] - lay + l
        specs.append(pl.BlockSpec((1, sw, cols), lambda i, end=end: (end, 0, 0)))
        specs.append(pl.BlockSpec((1, sw, cols), lambda i, l=l: (l, 0, 0)))
        flat += [later, got]
    return pl.pallas_call(
        apply_kernel,
        grid=(1,),
        in_specs=[pl.BlockSpec((sw, sw), lambda i: (0, 0))] + specs,
        out_specs=[pl.BlockSpec((1, sw, cols), lambda i: (0, 0, 0))] * 2,
        out_shape=[jax.ShapeDtypeStruct((1, sw, cols), jnp.float32)] * 2,
        compiler_params=SMALL,
        name="apply_factor",
    )(inv, *flat)


def finish_kernel(ranks_ref, *refs):
    o_ref = refs[-1]
    for l in range(o_ref.shape[0]):
        out = refs[2 * l][0] + refs[2 * l + 1][0]
        kept = lax.broadcasted_iota(jnp.int32, out.shape, 0) < ranks_ref[l]
        o_ref[l] = jnp.where(kept, out, 0.0)


def finish(ranks, pairs):
    _, sw, cols = pairs[0].shape
    return pl.pallas_call(
        finish_kernel,
        in_specs=[SCALARS] + [pl.BlockSpec((1, sw, cols), lambda: (0, 0, 0))] * len(pairs),
        out_shape=jax.ShapeDtypeStruct((len(pairs) // 2, sw, cols), jnp.float32),
        compiler_params=SMALL,
        name="finish",
    )(ranks, *pairs)


def shift(x, axis, size, k):
    return lax.ppermute(x, axis, [(i, (i + k) % size) for i in range(size)])


def added(parts):
    return sum(parts[1:], parts[0])


def ring_gather(arrays, axis, size):
    got = [{0: x} for x in arrays]
    up, down = list(arrays), list(arrays)
    for k in range(1, size // 2 + 1):
        for i in range(len(arrays)):
            got[i][k] = up[i] = shift(up[i], axis, size, -1)
            if k < size - k:
                got[i][size - k] = down[i] = shift(down[i], axis, size, 1)
    return [jnp.stack([g[k] for k in range(size)]) for g in got]


def per_device(planes, groups, lines, weights, coeffs, basis, sketch_map, ranks):
    lay = weights.shape[0]
    ys = groups // CORES
    pos = jnp.stack([lax.axis_index(a) for a in (*ROW, "x")]).astype(jnp.int32)
    near = jnp.stack([coeffs] + [shift(coeffs, "y", ys, k) for k in range(1, ys)])
    gathered = ring_gather((sketch_map, basis), "z", planes)
    all_maps, all_basis = [pltpu.with_memory_space_constraint(x, pltpu.HBM) for x in gathered]
    weights = pltpu.with_memory_space_constraint(weights, pltpu.HBM)
    (cut,) = after([near], [cut_by_owner(pos, weights, groups, planes)])
    others = shift(near, "c", CORES, 1)
    w = lax.all_to_all(cut, ("y", "c"), 0, 0, tiled=True)
    halves, residual, parts = 1, None, []
    for half in range(halves):
        residual, keep, send = residual_and_sketch(
            pos, half, halves, w, near, others, all_maps, all_basis, residual
        )
        got = shift(send, "c", CORES, 1)
        parts += [keep[i] + got[i] for i in range(ys // halves)]
    mine = added([parts[0]] + [shift(parts[k], "y", ys, -k) for k in range(1, ys)])
    mine = added([mine] + [shift(mine, "x", lines, k) for k in range(1, lines)])
    rows_near = jnp.stack([mine] + [shift(mine, "y", ys, k) for k in range(1, ys)])
    both, gram = stack_and_gram(pos, rows_near, shift(rows_near, "c", CORES, 1), lines)

    across = shift(gram, "z", planes, planes // 2)
    start = project(both, residual, 0, 1)
    later = project(both, residual, 1, planes // 2 - 1)
    gram = add_after(gram, across, start)
    start = after([gram], start)
    gram = ordered_sum(pos, [gram] + [shift(gram, "z", planes, k) for k in (1, 2, -1)], [])
    summed = gram
    gram = jnp.stack([gram] + [shift(gram, "x", lines, k) for k in range(1, lines)])
    other = shift(gram, "c", CORES, 1)

    def send_both(pair):
        return shift(pair[0], "z", planes, 1), shift(pair[1], "z", planes, -1)

    sent = ring_add(later, send_both(start), 0, [summed])
    sent = ring_add(later, send_both(sent), 1, [other])
    up, down = send_both(sent)
    upper = upper_factor(pos, gram, other, sent)
    inv = lower_factor(*upper, [])
    last0, last1 = apply_factor(inv, ((later[0], up), (later[1], down)))
    last0, last1 = shift(last0, "z", planes, 1), shift(last1, "z", planes, -1)
    rest0, rest1 = apply_factor(inv, ((later[1], down), (later[0], up)))
    ranks_here = lax.dynamic_slice_in_dim(ranks, lax.axis_index("x") * lay, lay)
    return finish(ranks_here, (last0, rest0, last1, rest1))


def solution(mesh):
    wide, lines = mesh.devices.shape
    groups = 8
    planes = wide // groups
    fine = Mesh(mesh.devices.reshape(planes, groups // CORES, CORES, lines), ROW + ("x",))
    in_specs = (
        P("x", ROW, None),
        P("x", ROW, None),
        P(None, ROW),
        P("x", ROW, None),
        P(),
    )
    return jax.shard_map(
        functools.partial(per_device, planes, groups, lines),
        mesh=fine,
        in_specs=in_specs,
        out_specs=P("x", None, ROW),
        check_vma=False,
    )
```

```python
import functools

import jax
import jax.numpy as jnp
from jax import lax
from jax.experimental import pallas as pl
from jax.experimental.pallas import tpu as pltpu
from jax.sharding import Mesh
from jax.sharding import PartitionSpec as P

ROW = ("z", "y", "c")
CORES = 2
STEP = 4
SMALL = pltpu.CompilerParams(vmem_limit_bytes=8 * 1024 * 1024)
LARGE = pltpu.CompilerParams(vmem_limit_bytes=24 * 1024 * 1024)
SCALARS = pl.BlockSpec(memory_space=pltpu.SMEM)
ANYWHERE = pl.BlockSpec(memory_space=pl.ANY)


def dot32(a, b, dims=((1,), (0,))):
    return lax.dot_general(
        a, b, (dims, ((), ())), precision=lax.Precision.HIGHEST, preferred_element_type=jnp.float32
    )


def cut_kernel(*refs):
    w_refs, o_ref = refs[1:-1], refs[-1]
    groups, cols = o_ref.shape[0], o_ref.shape[3] // len(w_refs)
    for i, w_ref in enumerate(w_refs):
        for g in range(groups):
            here = slice(g * cols, (g + 1) * cols)
            o_ref[g, :, :, i * cols : (i + 1) * cols] = w_ref[:, :, here]


def cut_by_owner(pos, weights, groups, planes):
    lay, rows, width = weights.shape
    cols = width // (groups * planes)
    ways = 4

    def place(i):
        return lambda z, pos: (0, 0, lax.rem(pos[0] + ways * z + i, planes))

    spec = pltpu.PrefetchScalarGridSpec(
        num_scalar_prefetch=1,
        grid=(planes // ways,),
        in_specs=[pl.BlockSpec((lay, rows, groups * cols), place(i)) for i in range(ways)],
        out_specs=pl.BlockSpec((groups, lay, rows, cols * ways), lambda z, pos: (0, 0, 0, z)),
    )
    return pl.pallas_call(
        cut_kernel,
        grid_spec=spec,
        out_shape=pltpu.HBM((groups, lay, rows, planes * cols), weights.dtype),
        compiler_params=LARGE,
        name="cut_by_owner",
    )(pos, *[weights] * ways)


def after_kernel(*refs):
    del refs


def after(first, arrays):
    return pl.pallas_call(
        after_kernel,
        in_specs=[ANYWHERE] * (len(arrays) + len(first)),
        out_specs=[ANYWHERE] * len(arrays),
        out_shape=[pltpu.HBM(a.shape, a.dtype) for a in arrays],
        input_output_aliases={i: i for i in range(len(arrays))},
        name="after",
    )(*arrays, *first)


def group_back(pos_ref, k, groups):
    lines = groups // CORES
    y = lax.rem(pos_ref[1] - k // CORES + lines, lines)
    c = lax.rem(pos_ref[2] + k % CORES, CORES)
    return y * CORES + c


def residual_kernel(count, _, *refs):
    w_refs, (c_ref, d_ref, b_ref, m_ref) = refs[:count], refs[count : count + 4]
    r_ref, keep_ref, send_ref, acc_ref, all_ref = refs[-5:]
    step, _, cols = b_ref.shape
    rows = w_refs[0].shape[2]
    layer, plane = pl.program_id(0), pl.program_id(1)

    @pl.when((layer == 0) & (plane == 0))
    def _():
        acc_ref[...] = jnp.zeros_like(acc_ref)

    @pl.when(plane == 0)
    def _():
        for k in range(count):
            all_ref[k * rows : (k + 1) * rows] = (c_ref, d_ref)[k % CORES][k // CORES, 0]

    total = None
    for i in range(step):
        here = slice(i * cols, (i + 1) * cols)
        low = jnp.dot(all_ref[...], b_ref[i], preferred_element_type=jnp.float32)
        w = jnp.concatenate([w_ref[0, 0, :, here] for w_ref in w_refs], axis=0)
        res = (w.astype(jnp.float32) - low).astype(jnp.bfloat16)
        r_ref[0, i] = res
        part = jnp.dot(res, m_ref[i, 0], preferred_element_type=jnp.float32)
        total = part if total is None else total + part
    acc_ref[...] += total

    @pl.when((layer == pl.num_programs(0) - 1) & (plane == pl.num_programs(1) - 1))
    def _():
        for k in range(count):
            (keep_ref, send_ref)[k % CORES][k // CORES] = acc_ref[k * rows : (k + 1) * rows]


def residual_and_sketch(pos, half, halves, w, near, others, maps, basis, before):
    groups, lay, rows, width = w.shape
    count = groups // halves
    planes, _, _, sw = maps.shape
    rank = near.shape[3]
    cols = width // planes
    tall = count * rows
    coeff = pl.BlockSpec((count // CORES, 1, rows, rank), lambda l, z, pos: (half, l, 0, 0))
    kept = [] if before is None else [before]

    def place(k):
        return lambda l, z, pos: (group_back(pos, half * count + k, groups), l, 0, z)

    spec = pltpu.PrefetchScalarGridSpec(
        num_scalar_prefetch=1,
        grid=(lay, planes // STEP),
        in_specs=[pl.BlockSpec((1, 1, rows, cols * STEP), place(k)) for k in range(count)]
        + [
            coeff,
            coeff,
            pl.BlockSpec((STEP, rank, cols), lambda l, z, pos: (z, 0, 0)),
            pl.BlockSpec((STEP, 1, cols, sw), lambda l, z, pos: (z, l, 0, 0)),
        ]
        + [ANYWHERE] * len(kept),
        out_specs=[pl.BlockSpec((1, STEP, tall, cols), lambda l, z, pos: (l, z, half, 0))]
        + [pl.BlockSpec((count // CORES, rows, sw), lambda l, z, pos: (0, 0, 0))] * CORES,
        scratch_shapes=[
            pltpu.VMEM((tall, sw), jnp.float32),
            pltpu.VMEM((tall, rank), jnp.bfloat16),
        ],
    )
    return pl.pallas_call(
        functools.partial(residual_kernel, count),
        grid_spec=spec,
        out_shape=[jax.ShapeDtypeStruct((lay, planes, halves * tall, cols), jnp.bfloat16)]
        + [jax.ShapeDtypeStruct((count // CORES, rows, sw), jnp.float32)] * CORES,
        input_output_aliases={count + 5: 0} if kept else {},
        compiler_params=LARGE,
        name="residual_and_sketch",
    )(pos, *[w] * count, near, others, basis, maps, *kept)


def gram_kernel(pos_ref, near_ref, other_ref, both_ref, g_ref, t_ref):
    ys = near_ref.shape[0]
    sketch = [ref[k] for k in range(ys) for ref in (near_ref, other_ref)]
    sketch = jnp.concatenate(sketch, axis=0)
    share, sw = g_ref.shape
    t_ref[...] = sketch.T
    at = pl.multiple_of((pos_ref[3] * CORES + pos_ref[2]) * share, share)
    g_ref[...] = dot32(t_ref[pl.ds(at, share)], sketch)
    high = t_ref[...].astype(jnp.bfloat16)
    both_ref[:sw] = high
    both_ref[sw:] = (t_ref[...] - high.astype(jnp.float32)).astype(jnp.bfloat16)


def stack_and_gram(pos, near, others, lines):
    ys, rows, sw = near.shape
    tall = rows * ys * CORES
    return pl.pallas_call(
        gram_kernel,
        in_specs=[SCALARS] + [pl.BlockSpec(near.shape, lambda: (0, 0, 0))] * CORES,
        out_shape=[
            jax.ShapeDtypeStruct((2 * sw, tall), jnp.bfloat16),
            jax.ShapeDtypeStruct((sw // (CORES * lines), sw), jnp.float32),
        ],
        scratch_shapes=[pltpu.VMEM((sw, tall), jnp.float32)],
        compiler_params=SMALL,
        name="stack_and_gram",
    )(pos, near, others)


def project_kernel(both_ref, *refs):
    r_refs, o_refs = refs[:4], refs[4:]
    sw = both_ref.shape[0] // 2
    for i, r_ref in enumerate(r_refs):
        out = jnp.dot(both_ref[...], r_ref[0, 0], preferred_element_type=jnp.float32)
        o_refs[i % 2][i // 2] = out[:sw] + out[sw:]


def project(both, residual, first, rounds):
    lay, planes, rows, cols = residual.shape
    sw = both.shape[0] // 2
    mid = planes // 2
    places = (
        lambda r: (0, mid - first - r, 0, 0),
        lambda r: (0, lax.rem(mid + 1 + first + r, planes), 0, 0),
        lambda r: (1, mid - 1 - first - r, 0, 0),
        lambda r: (1, mid + first + r, 0, 0),
    )
    return pl.pallas_call(
        project_kernel,
        grid=(rounds,),
        in_specs=[pl.BlockSpec(both.shape, lambda r: (0, 0))]
        + [pl.BlockSpec((1, 1, rows, cols), place) for place in places],
        out_specs=[pl.BlockSpec((lay, sw, cols), lambda r: (r, 0, 0))] * 2,
        out_shape=[jax.ShapeDtypeStruct((rounds * lay, sw, cols), jnp.float32)] * 2,
        compiler_params=LARGE,
        name="project",
    )(both, *[residual] * len(places))


def factor_block(a):
    n = a.shape[0]
    four = 4
    row = lax.broadcasted_iota(jnp.int32, (n, n), 0)
    col = lax.broadcasted_iota(jnp.int32, (n, n), 1)
    left, right = a, jnp.where(row == col, 1.0, 0.0)
    done = []
    for j in range(0, n, four):
        r = j % 8
        if j and r == 0:
            left, right = left[8:], right[8:]
        mults = [
            jnp.broadcast_to(left[:, j + k : j + k + 1], left.shape) for k in range(four)
        ]
        lines = []
        for k in range(four):
            here = slice(r + k, r + k + 1)
            lower, upper = left[here], right[here]
            mult = mults[k]
            for m, (done_left, done_right) in enumerate(lines):
                weight = mults[m][here]
                lower = lower - weight * done_left
                upper = upper - weight * done_right
                mult = mult - mults[m] * mults[m][here]
            pivot = lax.rsqrt(mult[here])
            mults[k] = mult * pivot
            lines.append((lower * pivot, upper * pivot))
        for k in range(four):
            left = left - mults[k] * lines[k][0]
            right = right - mults[k] * lines[k][1]
            done.append(lines[k][1])
    return jnp.concatenate(done, axis=0)


def upper_kernel(pos_ref, mine_ref, other_ref, *refs):
    inv_ref, cross_ref, rest_ref, g_ref = refs[-4:]
    lines, share, _ = mine_ref.shape
    half = inv_ref.shape[0]
    for k in range(lines):
        x = lax.rem(pos_ref[3] - k + lines, lines) * CORES
        for c, ref in ((pos_ref[2], mine_ref), (1 - pos_ref[2], other_ref)):
            g_ref[pl.ds(pl.multiple_of((x + c) * share, share), share)] = ref[k]
    inv = factor_block(g_ref[:half, :half])
    panel = dot32(g_ref[half:, :half], inv, ((1,), (1,)))
    inv_ref[...] = inv
    cross_ref[...] = dot32(panel, inv)
    rest_ref[...] = g_ref[half:, half:] - dot32(panel, panel, ((1,), (1,)))


def upper_factor(pos, mine, other, first):
    lines, share, sw = mine.shape
    half = sw // 2
    return pl.pallas_call(
        upper_kernel,
        in_specs=[SCALARS]
        + [pl.BlockSpec(mine.shape, lambda: (0, 0, 0))] * 2
        + [ANYWHERE] * len(first),
        out_shape=[jax.ShapeDtypeStruct((half, half), jnp.float32)] * 3,
        scratch_shapes=[pltpu.VMEM((sw, sw), jnp.float32)],
        compiler_params=SMALL,
        name="upper_factor",
    )(pos, mine, other, *first)


def lower_kernel(inv_ref, cross_ref, rest_ref, *refs):
    o_ref = refs[-1]
    half = inv_ref.shape[0]
    inv = factor_block(rest_ref[...])
    o_ref[:half, :half] = inv_ref[...]
    o_ref[:half, half:] = jnp.zeros_like(inv)
    o_ref[half:, :half] = -dot32(inv, cross_ref[...])
    o_ref[half:, half:] = inv


def lower_factor(inv, cross, rest, first):
    full = 2 * inv.shape[0]
    return pl.pallas_call(
        lower_kernel,
        in_specs=[pl.BlockSpec(inv.shape, lambda: (0, 0))] * 3 + [ANYWHERE] * len(first),
        out_shape=jax.ShapeDtypeStruct((full, full), jnp.float32),
        compiler_params=SMALL,
        name="lower_factor",
    )(inv, cross, rest, *first)


def sum_kernel(*refs):
    refs[-1][...] = refs[0][...] + refs[1][...]


def add_after(a, b, first):
    whole = pl.BlockSpec(a.shape, lambda: (0, 0))
    return pl.pallas_call(
        sum_kernel,
        in_specs=[whole] * 2 + [ANYWHERE] * len(first),
        out_specs=whole,
        out_shape=jax.ShapeDtypeStruct(a.shape, a.dtype),
        compiler_params=SMALL,
        name="add_after",
    )(a, b, *first)


def ordered_kernel(n, pos_ref, *refs):
    parts, (o_ref, all_ref) = refs[:n], refs[-2:]
    for k, ref in enumerate(parts):
        all_ref[lax.rem(pos_ref[0] - k + 2 * n, n)] = ref[...]
    total = all_ref[0]
    for k in range(1, n):
        total = total + all_ref[k]
    o_ref[...] = total


def ordered_sum(pos, parts, first):
    shape = parts[0].shape
    return pl.pallas_call(
        functools.partial(ordered_kernel, len(parts)),
        in_specs=[SCALARS]
        + [pl.BlockSpec(shape, lambda: (0, 0))] * len(parts)
        + [ANYWHERE] * len(first),
        out_shape=jax.ShapeDtypeStruct(shape, jnp.float32),
        scratch_shapes=[pltpu.VMEM((len(parts), *shape), jnp.float32)],
        compiler_params=SMALL,
        name="ordered_sum",
    )(pos, *parts, *first)


def add_kernel(*refs):
    refs[-2][...] = refs[0][...] + refs[2][...]
    refs[-1][...] = refs[1][...] + refs[3][...]


def ring_add(later, got, r, first):
    rounds, (lay, sw, cols) = later[0].shape[0] // got[0].shape[0], got[0].shape
    one = r == rounds - 1
    n = 1 if one else lay
    where = (0, 1) if one else (0, 0)
    return pl.pallas_call(
        add_kernel,
        grid=(1,),
        in_specs=[pl.BlockSpec((n, sw, cols), lambda i, w=w: (lay // n * r + w, 0, 0)) for w in where]
        + [pl.BlockSpec((n, sw, cols), lambda i, w=w: (w, 0, 0)) for w in where]
        + [ANYWHERE] * len(first),
        out_specs=[pl.BlockSpec((n, sw, cols), lambda i: (0, 0, 0))] * 2,
        out_shape=[jax.ShapeDtypeStruct((n, sw, cols), jnp.float32)] * 2,
        compiler_params=SMALL,
        name="ring_add",
    )(*later, *got, *first)


def apply_kernel(inv_ref, *refs):
    for i in range(2):
        refs[4 + i][0] = dot32(inv_ref[...], refs[2 * i][0] + refs[2 * i + 1][0])


def apply_factor(inv, pairs):
    specs, flat = [], []
    for l, (later, got) in enumerate(pairs):
        lay, sw, cols = got.shape
        end = later.shape[0] - lay + l
        specs.append(pl.BlockSpec((1, sw, cols), lambda i, end=end: (end, 0, 0)))
        specs.append(pl.BlockSpec((1, sw, cols), lambda i, l=l: (l, 0, 0)))
        flat += [later, got]
    return pl.pallas_call(
        apply_kernel,
        grid=(1,),
        in_specs=[pl.BlockSpec((sw, sw), lambda i: (0, 0))] + specs,
        out_specs=[pl.BlockSpec((1, sw, cols), lambda i: (0, 0, 0))] * 2,
        out_shape=[jax.ShapeDtypeStruct((1, sw, cols), jnp.float32)] * 2,
        compiler_params=SMALL,
        name="apply_factor",
    )(inv, *flat)


def finish_kernel(ranks_ref, *refs):
    o_ref = refs[-1]
    for l in range(o_ref.shape[0]):
        out = refs[2 * l][0] + refs[2 * l + 1][0]
        kept = lax.broadcasted_iota(jnp.int32, out.shape, 0) < ranks_ref[l]
        o_ref[l] = jnp.where(kept, out, 0.0)


def finish(ranks, pairs):
    _, sw, cols = pairs[0].shape
    return pl.pallas_call(
        finish_kernel,
        in_specs=[SCALARS] + [pl.BlockSpec((1, sw, cols), lambda: (0, 0, 0))] * len(pairs),
        out_shape=jax.ShapeDtypeStruct((len(pairs) // 2, sw, cols), jnp.float32),
        compiler_params=SMALL,
        name="finish",
    )(ranks, *pairs)


def shift(x, axis, size, k):
    return lax.ppermute(x, axis, [(i, (i + k) % size) for i in range(size)])


def added(parts):
    return sum(parts[1:], parts[0])


def ring_gather(arrays, axis, size):
    got = [{0: x} for x in arrays]
    up, down = list(arrays), list(arrays)
    for k in range(1, size // 2 + 1):
        for i in range(len(arrays)):
            got[i][k] = up[i] = shift(up[i], axis, size, -1)
            if k < size - k:
                got[i][size - k] = down[i] = shift(down[i], axis, size, 1)
    return [jnp.stack([g[k] for k in range(size)]) for g in got]


def per_device(planes, groups, lines, weights, coeffs, basis, sketch_map, ranks):
    lay = weights.shape[0]
    ys = groups // CORES
    pos = jnp.stack([lax.axis_index(a) for a in (*ROW, "x")]).astype(jnp.int32)
    near = jnp.stack([coeffs] + [shift(coeffs, "y", ys, k) for k in range(1, ys)])
    gathered = ring_gather((sketch_map, basis), "z", planes)
    all_maps, all_basis = [pltpu.with_memory_space_constraint(x, pltpu.HBM) for x in gathered]
    weights = pltpu.with_memory_space_constraint(weights, pltpu.HBM)
    (cut,) = after([near], [cut_by_owner(pos, weights, groups, planes)])
    others = shift(near, "c", CORES, 1)
    w = lax.all_to_all(cut, ("y", "c"), 0, 0, tiled=True)
    halves, residual, parts = 1, None, []
    for half in range(halves):
        residual, keep, send = residual_and_sketch(
            pos, half, halves, w, near, others, all_maps, all_basis, residual
        )
        got = shift(send, "c", CORES, 1)
        parts += [keep[i] + got[i] for i in range(ys // halves)]
    mine = added([parts[0]] + [shift(parts[k], "y", ys, -k) for k in range(1, ys)])
    mine = added([mine] + [shift(mine, "x", lines, k) for k in range(1, lines)])
    rows_near = jnp.stack([mine] + [shift(mine, "y", ys, k) for k in range(1, ys)])
    both, gram = stack_and_gram(pos, rows_near, shift(rows_near, "c", CORES, 1), lines)

    across = shift(gram, "z", planes, planes // 2)
    start = project(both, residual, 0, 1)
    later = project(both, residual, 1, planes // 2 - 1)
    gram = add_after(gram, across, start)
    start = after([across], start)
    gram = ordered_sum(pos, [gram] + [shift(gram, "z", planes, k) for k in (1, 2, -1)], [])
    summed = gram
    gram = jnp.stack([gram] + [shift(gram, "x", lines, k) for k in range(1, lines)])
    other = shift(gram, "c", CORES, 1)

    def send_both(pair):
        return shift(pair[0], "z", planes, 1), shift(pair[1], "z", planes, -1)

    sent = ring_add(later, send_both(start), 0, [summed])
    sent = ring_add(later, send_both(sent), 1, [other])
    up, down = send_both(sent)
    upper = upper_factor(pos, gram, other, sent)
    inv = lower_factor(*upper, [])
    last0, last1 = apply_factor(inv, ((later[0], up), (later[1], down)))
    last0, last1 = shift(last0, "z", planes, 1), shift(last1, "z", planes, -1)
    rest0, rest1 = apply_factor(inv, ((later[1], down), (later[0], up)))
    ranks_here = lax.dynamic_slice_in_dim(ranks, lax.axis_index("x") * lay, lay)
    return finish(ranks_here, (last0, rest0, last1, rest1))


def solution(mesh):
    wide, lines = mesh.devices.shape
    groups = 8
    planes = wide // groups
    fine = Mesh(mesh.devices.reshape(planes, groups // CORES, CORES, lines), ROW + ("x",))
    in_specs = (
        P("x", ROW, None),
        P("x", ROW, None),
        P(None, ROW),
        P("x", ROW, None),
        P(),
    )
    return jax.shard_map(
        functools.partial(per_device, planes, groups, lines),
        mesh=fine,
        in_specs=in_specs,
        out_specs=P("x", None, ROW),
        check_vma=False,
    )
```
